256 devices in a mesh: dp: 8 (over x, z_hi), tensor: 32 (over z_lo, y, core).
Axes of the slice: x: 4, y: 4, z: 8 (z_hi: 2, z_lo: 4; z = z_hi * 4 + z_lo), core: 2. Of those that a mesh axis runs over, the one named last changes fastest.
Arguments:
- tokens: bfloat16 [2048, 4096], P('dp', 'tensor'), may hold values from -6 to 6
- cotangent: bfloat16 [2048, 4096], P('dp', 'tensor'), may hold values from -6 to 6
- gu_master: float32 [2, 4096, 8192], P(None, 'dp', 'tensor'), may hold values from -0.09375 to 0.09375
- gu_first: float32 [2, 4096, 8192], P(None, 'dp', 'tensor'), may hold values from -0.046875 to 0.046875
- gu_second: float32 [2, 4096, 8192], P(None, 'dp', 'tensor'), may hold values from 1e-06 to 0.0001
- gu_codes: int32 [2, 1024, 8192], P(None, 'dp', 'tensor'), may hold values from 0 to 5
- gu_expo: int32 [2, 8192], P(None, 'tensor'), may hold values from -6 to -4
- down_master: float32 [8192, 4096], P('tensor', 'dp'), may hold values from -0.0625 to 0.0625
- down_first: float32 [8192, 4096], P('tensor', 'dp'), may hold values from -0.046875 to 0.046875
- down_second: float32 [8192, 4096], P('tensor', 'dp'), may hold values from 1e-06 to 0.0001
- down_codes: int32 [2048, 4096], P('tensor', 'dp'), may hold values from 0 to 5
- down_expo: int32 [4096], P('dp'), may hold values from -7 to -5
Outputs:
- mixed: bfloat16 [2048, 4096], P('dp', 'tensor')
- token_grad: bfloat16 [2048, 4096], P('dp', 'tensor')
- gu_new: float32 [2, 4096, 8192], P(None, 'dp', 'tensor')
- gu_first_new: float32 [2, 4096, 8192], P(None, 'dp', 'tensor')
- gu_second_new: float32 [2, 4096, 8192], P(None, 'dp', 'tensor')
- gu_copy: bfloat16 [2, 4096, 8192], P(None, 'dp', 'tensor')
- down_new: float32 [8192, 4096], P('tensor', 'dp')
- down_first_new: float32 [8192, 4096], P('tensor', 'dp')
- down_second_new: float32 [8192, 4096], P('tensor', 'dp')
- down_copy: bfloat16 [8192, 4096], P('tensor', 'dp')
The draws below stay inside these ranges and needn't reach their ends.
Inputs may be any that keep to these rules, and one draw needn't show every extreme that they name: `gu_codes`: code of which two of the four rows of a group are kept: 0 (0,1), 1 (0,2), 2 (0,3), 3 (1,2), 4 (1,3), 5 (2,3). `down_codes`: code of which two of the four hidden units of a group are kept, numbered as for gu_codes.
All inputs are finite; a program needn't handle non-finite values.
Results may differ from the reference program's by a relative error of at most 0.03.
Values may be sent and summed in bfloat16 or wider, within the bound.
No kernel may reach another device: no remote copies, remote signals or barrier semaphores. Data moves between devices by JAX's collectives and lax.ppermute only.
A program may use at most 128 MiB of HBM per device.

```python
import math
import jax
import jax.numpy as jnp
from jax import lax

D = 4096
FF = 8192
TOKENS_PER_SHARD = 256
TOKENS = 2048
N_DP = 8
N_TENSOR = 32


def with_ends(values, stream_key, smallest, high):
    shape = values.shape
    index_at = [jax.random.randint(jax.random.fold_in(stream_key, axis), (), 0, shape[axis]) for axis in range(len(shape))]
    values = values.at[tuple(index_at)].set(smallest)
    longest = shape.index(max(shape))
    index_at[longest] = (index_at[longest] + 1) % shape[longest]
    return values.at[tuple(index_at)].set(high)


def spiked(values, rng, source, target, blocks, factor):
    def block_of(dim):
        return (jnp.arange(values.shape[dim]) // (values.shape[dim] // blocks)).reshape((-1,) + (1,) * (values.ndim - 1 - dim))

    one_side = jax.random.permutation(rng, blocks)[block_of(target)]
    second = (block_of(target) + blocks // 2) % blocks
    return jnp.where((block_of(source) == one_side) | (block_of(source) == second), factor * values, values)


def level_of(own_key, dims, split, low, largest):
    factor_of, own = 1.0, jax.random.fold_in(own_key, 6)
    for axis_at, blocks in split:
        heights = jnp.exp(jax.random.uniform(jax.random.fold_in(own, axis_at), (blocks,), jnp.float32, low / len(split), largest / len(split)))
        factor_of = factor_of * jnp.repeat(heights, dims[axis_at] // blocks).reshape([-1 if axis == axis_at else 1 for axis in range(len(dims))])
    return factor_of


def scatter_about(rng, extent, spread, most, pieces=(), held_as=jnp.bfloat16):
    gain = level_of(rng, extent, pieces, -0.22, 0.18) if pieces else 1.0
    values = jax.random.normal(rng, extent, jnp.float32) * spread * gain
    return jnp.minimum(jnp.maximum(values, -most), most).astype(held_as)


def heavy_noise(key, dims, width, limit, shards, heavy, kind=jnp.bfloat16):
    values = width * jax.random.normal(key, dims, jnp.float32)
    if shards:
        values = values * level_of(key, dims, shards, -0.22, 0.18)
    return jnp.clip(spiked(values, jax.random.fold_in(key, 3), *heavy), -limit, limit).astype(kind)


def setup_inputs(seed: int = 0) -> dict:
    streams_of = jax.random.split(jax.random.key(seed), 13)
    return {
        "tokens": heavy_noise(streams_of[0], (TOKENS, D), 1.0, 6.0, ((0, 8), (1, 32)), (0, 1, 32, 2.75)),
        "cotangent": heavy_noise(streams_of[1], (TOKENS, D), 1.0, 6.0, ((0, 8), (1, 32)), (0, 1, 32, 2.75)),
        "gu_master": scatter_about(streams_of[2], (2, D, FF), D ** -0.5, 0.09375, ((1, 8), (2, 32)), jnp.float32),
        "gu_first": scatter_about(streams_of[3], (2, D, FF), 0.003, 0.046875, ((1, 8), (2, 32)), jnp.float32),
        "gu_second": jnp.clip(jnp.exp(math.log(0.0001) - 4.6051702 * jax.random.uniform(streams_of[4], (2, D, FF), jnp.float32) ** level_of(streams_of[4], (2, D, FF), ((1, 8), (2, 32)), -0.2, 0.2)), 9.999999974752427e-07, 0.0001),
        "gu_codes": with_ends(jax.random.randint(streams_of[5], (2, D // 4, FF), 0, 6), jax.random.fold_in(streams_of[5], 1), 0, 5).astype(jnp.int32),
        "gu_expo": with_ends(jax.random.randint(streams_of[6], (2, FF), -6, -3), jax.random.fold_in(streams_of[6], 1), -6, (-3) - 1).astype(jnp.int32),
        "down_master": scatter_about(streams_of[7], (FF, D), FF ** -0.5, 0.0625, ((0, 32), (1, 8)), jnp.float32),
        "down_first": scatter_about(streams_of[8], (FF, D), 0.003, 0.046875, ((0, 32), (1, 8)), jnp.float32),
        "down_second": jnp.clip(jnp.exp(math.log(0.0001) - 4.6051702 * jax.random.uniform(streams_of[9], (FF, D), jnp.float32) ** level_of(streams_of[9], (FF, D), ((0, 32), (1, 8)), -0.2, 0.2)), 9.999999974752427e-07, 0.0001),
        "down_codes": with_ends(jax.random.randint(streams_of[10], (FF // 4, D), 0, 6), jax.random.fold_in(streams_of[10], 1), 0, 5).astype(jnp.int32),
        "down_expo": with_ends(jax.random.randint(streams_of[11], (D,), -7, -4), jax.random.fold_in(streams_of[11], 1), -7, (-4) - 1).astype(jnp.int32),
    }


BETA_ONE = 0.9
BETA_TWO = 0.95
ADAM_EPS = 1e-08
LEARN_RATE = 0.002
CORRECT_ONE = 1.0 - 0.9 ** 10
CORRECT_TWO = 1.0 - 0.95 ** 10

def power_of_two(expo):
    result = jnp.zeros(expo.shape, jnp.float32)
    for level in range(-8, 0):
        result = jnp.where(expo == level, jnp.float32(2.0 ** level), result)
    return result

def expand_codes(codes):
    first = jnp.where(codes < 3, 0, jnp.where(codes < 5, 1, 2))
    second = jnp.where(codes == 0, 1, jnp.where((codes == 1) | (codes == 3), 2, 3))
    place = jnp.arange(4, dtype=jnp.int32).reshape(4, 1)
    keeper = (place == first[..., :, None, :]) | (place == second[..., :, None, :])
    shape = codes.shape[:-2] + (codes.shape[-2] * 4, codes.shape[-1])
    return keeper.reshape(shape).astype(jnp.float32)

def quantize(master, keeper, scale):
    inner = jnp.clip(master / scale, -1.0, 1.0) * keeper
    return inner.astype(jnp.bfloat16) * scale.astype(jnp.bfloat16)

def adam_update(master, first, second, grad):
    first = BETA_ONE * first + (1.0 - BETA_ONE) * grad
    second = BETA_TWO * second + (1.0 - BETA_TWO) * grad * grad
    update = first / CORRECT_ONE / (jnp.sqrt(second / CORRECT_TWO) + ADAM_EPS)
    return (master - LEARN_RATE * update, first, second)

def rounded_values(value):
    return lax.optimization_barrier(value.astype(jnp.bfloat16)).astype(jnp.float32)

def reference(tokens, cotangent, gu_master, gu_first, gu_second, gu_codes, gu_expo, down_master, down_first, down_second, down_codes, down_expo):
    gu_keep = expand_codes(gu_codes)
    gu_scale = power_of_two(gu_expo)[:, None, :]
    dn_keep = expand_codes(down_codes)
    dn_scale = power_of_two(down_expo)[None, :]
    gu_quant = quantize(gu_master, gu_keep, gu_scale)
    down_quant = quantize(down_master, dn_keep, dn_scale)
    gate = jnp.dot(tokens, gu_quant[0], preferred_element_type=jnp.float32)
    up = jnp.dot(tokens, gu_quant[1], preferred_element_type=jnp.float32)
    sig = jax.nn.sigmoid(gate)
    act = gate * sig
    hidden_state = (act * up).astype(jnp.bfloat16)
    block = FF // N_TENSOR

    def out_step(index, total):
        start_offset = (index * block).astype(jnp.int32)
        hid = lax.dynamic_slice_in_dim(hidden_state, start_offset, block, 1)
        wts = lax.dynamic_slice_in_dim(down_quant, start_offset, block, 0)
        return total + rounded_values(jnp.dot(hid, wts, preferred_element_type=jnp.float32))
    mixed = lax.fori_loop(0, N_TENSOR, out_step, jnp.zeros((TOKENS, D), jnp.float32)).astype(jnp.bfloat16)
    dhid = jnp.dot(cotangent, down_quant.T, preferred_element_type=jnp.float32)
    dgate = (dhid * up * sig * (1.0 + gate * (1.0 - sig))).astype(jnp.bfloat16)
    dup = (dhid * act).astype(jnp.bfloat16)

    def in_step(index, total):
        start_offset = (index * block).astype(jnp.int32)
        dgk = lax.dynamic_slice_in_dim(dgate, start_offset, block, 1)
        duk = lax.dynamic_slice_in_dim(dup, start_offset, block, 1)
        gqk = lax.dynamic_slice_in_dim(gu_quant[0], start_offset, block, 1)
        uqk = lax.dynamic_slice_in_dim(gu_quant[1], start_offset, block, 1)
        term = jnp.dot(dgk, gqk.T, preferred_element_type=jnp.float32) + jnp.dot(duk, uqk.T, preferred_element_type=jnp.float32)
        return total + rounded_values(term)
    token_grad = lax.fori_loop(0, N_TENSOR, in_step, jnp.zeros((TOKENS, D), jnp.float32)).astype(jnp.bfloat16)
    inverse_scale = 1.0 / TOKENS

    def grad_step(index, totals):
        start_offset = (index * TOKENS_PER_SHARD).astype(jnp.int32)
        tok = lax.dynamic_slice_in_dim(tokens, start_offset, TOKENS_PER_SHARD, 0)
        output_cotangent = lax.dynamic_slice_in_dim(cotangent, start_offset, TOKENS_PER_SHARD, 0)
        dgb = lax.dynamic_slice_in_dim(dgate, start_offset, TOKENS_PER_SHARD, 0)
        dub = lax.dynamic_slice_in_dim(dup, start_offset, TOKENS_PER_SHARD, 0)
        hidden_bfloat = lax.dynamic_slice_in_dim(hidden_state, start_offset, TOKENS_PER_SHARD, 0)
        g_gate = rounded_values(jnp.dot(tok.T, dgb, preferred_element_type=jnp.float32) * inverse_scale)
        g_up = rounded_values(jnp.dot(tok.T, dub, preferred_element_type=jnp.float32) * inverse_scale)
        down_weight_grad = rounded_values(jnp.dot(hidden_bfloat.T, output_cotangent, preferred_element_type=jnp.float32) * inverse_scale)
        return (totals[0] + g_gate, totals[1] + g_up, totals[2] + down_weight_grad)
    zero_gu = jnp.zeros((D, FF), jnp.float32)
    grad_gate, grad_up, grad_down = lax.fori_loop(0, N_DP, grad_step, (zero_gu, zero_gu, jnp.zeros((FF, D), jnp.float32)))
    gu_inside = (jnp.abs(gu_master / gu_scale) <= 1.0).astype(jnp.float32)
    dn_inside = (jnp.abs(down_master / dn_scale) <= 1.0).astype(jnp.float32)
    gu_grad = jnp.stack([grad_gate, grad_up]) * gu_keep * gu_inside
    dn_grad = grad_down * dn_keep * dn_inside
    gu_new, gu_first_new, gu_second_new = adam_update(gu_master, gu_first, gu_second, gu_grad)
    down_new, down_first_new, down_second_new = adam_update(down_master, down_first, down_second, dn_grad)
    gu_copy = quantize(gu_new, gu_keep, gu_scale)
    down_copy = quantize(down_new, dn_keep, dn_scale)
    return (mixed, token_grad, gu_new, gu_first_new, gu_second_new, gu_copy, down_new, down_first_new, down_second_new, down_copy)
```

```python
import jax
import jax.numpy as jnp
from jax import lax
from jax.experimental import pallas as pl
from jax.experimental.pallas import tpu as pltpu
from jax.sharding import PartitionSpec as P

BETA_ONE = 0.9
BETA_TWO = 0.95
ADAM_EPS = 1e-08
LEARN_RATE = 0.002
CORRECT_ONE = 1.0 - 0.9**10
CORRECT_TWO = 1.0 - 0.95**10

ALL = ("dp", "tensor")
F32 = jnp.float32
BF16 = jnp.bfloat16
VMEM = pl.BlockSpec(memory_space=pltpu.VMEM)
SMEM = pl.BlockSpec(memory_space=pltpu.SMEM)
X_GROUPS = [[hi + 2 * x for x in range(4)] for hi in range(2)]
Y_OFFSETS = (0, 3, 1, 2)


def device_number(x, hi, lo, y, core):
    return (x * 2 + hi) * 32 + lo * 8 + y * 2 + core


def move(value, target):
    pairs = []
    for x in range(4):
        for hi in range(2):
            for lo in range(4):
                for y in range(4):
                    for core in range(2):
                        here = device_number(x, hi, lo, y, core)
                        pairs.append((here, device_number(*target(x, hi, lo, y, core))))
    return lax.ppermute(value, ALL, pairs)


def along_y(step):
    return lambda x, hi, lo, y, core: (x, hi, lo, (y + step) % 4, core)


def along_lo(step):
    return lambda x, hi, lo, y, core: (x, hi, (lo + step) % 4, y, core)


def other_hi(x, hi, lo, y, core):
    return (x, 1 - hi, lo, y, core)


def other_core(x, hi, lo, y, core):
    return (x, hi, lo, y, 1 - core)


def swap_hi_y(x, hi, lo, y, core):
    return (x, y >> 1, lo, hi * 2 + (y & 1), core)


def power_of_two(expo, sign):
    result = jnp.zeros(expo.shape, F32)
    for level in range(-8, 0):
        result = jnp.where(expo == level, jnp.float32(2.0 ** (sign * level)), result)
    return result


def expand_codes(codes):
    groups = codes.shape[0]
    rows = groups * 4
    spread = (
        (lax.broadcasted_iota(jnp.int32, (rows, groups), 0) >> 2)
        == lax.broadcasted_iota(jnp.int32, (rows, groups), 1)
    ).astype(F32).astype(BF16)
    code = jnp.dot(spread, codes.astype(F32).astype(BF16), preferred_element_type=F32)
    place = (lax.broadcasted_iota(jnp.int32, code.shape, 0) & 3).astype(F32)
    first = jnp.where(code < 2.5, 0.0, jnp.where(code < 4.5, 1.0, 2.0))
    second = jnp.where(
        code == 0.0, 1.0, jnp.where((code == 1.0) | (code == 3.0), 2.0, 3.0)
    )
    return ((place == first) | (place == second)).astype(F32)


def quantize(master, keeper, scale, inverse):
    inner = jnp.clip(master * inverse, -1.0, 1.0) * keeper
    return inner.astype(BF16) * scale.astype(BF16)


def quantize_kernel(gu_ref, gu_codes, gu_expo, dn_ref, dn_codes, dn_expo, out_ref):
    for part in range(2):
        expo = gu_expo[part : part + 1, :]
        out_ref[part] = quantize(
            gu_ref[part],
            expand_codes(gu_codes[part]),
            power_of_two(expo, 1),
            power_of_two(expo, -1),
        )
    expo = dn_expo[...]
    down = jnp.clip(dn_ref[...] * power_of_two(expo, -1), -1.0, 1.0) * expand_codes(dn_codes[...])
    down = down.astype(BF16) * power_of_two(expo, 1).astype(BF16)
    out_ref[2] = down.astype(F32).T.astype(BF16)


def adam(master, first, second, grad, codes, expo):
    keeper = expand_codes(codes)
    inverse = power_of_two(expo, -1)
    inside = (jnp.abs(master * inverse) <= 1.0).astype(F32)
    grad = grad * keeper * inside
    first = BETA_ONE * first + (1.0 - BETA_ONE) * grad
    second = BETA_TWO * second + (1.0 - BETA_TWO) * grad * grad
    update = first / CORRECT_ONE / (jnp.sqrt(second / CORRECT_TWO) + ADAM_EPS)
    master = master - LEARN_RATE * update
    return master, first, second, quantize(master, keeper, power_of_two(expo, 1), inverse)


def gu_adam_kernel(grad, master, first, second, codes, expo, new, new_first, new_second, copy):
    which = pl.program_id(0)
    chosen = jnp.where(which == 0, expo[0:1, :], expo[1:2, :])
    result = adam(
        master[0], first[0], second[0], grad[0].astype(F32), codes[0], chosen
    )
    new[0], new_first[0], new_second[0], copy[0] = result


def down_adam_kernel(grad, master, first, second, codes, expo, new, new_first, new_second, copy):
    result = adam(
        master[...], first[...], second[...], grad[0].astype(F32).T, codes[...], expo[...]
    )
    new[...], new_first[...], new_second[...], copy[...] = result


def gu_update(grads, master, first, second, codes, expo):
    parts, rows, cols = master.shape
    size = rows // 2
    block = pl.BlockSpec((1, size, cols), lambda i, j: (i, j, 0))
    narrow = pl.BlockSpec((1, size // 4, cols), lambda i, j: (i, j, 0))
    whole = pl.BlockSpec((parts, cols), lambda i, j: (0, 0))
    like = jax.ShapeDtypeStruct(master.shape, F32)
    return pl.pallas_call(
        gu_adam_kernel,
        grid=(parts, 2),
        in_specs=[block, block, block, block, narrow, whole],
        out_specs=[block] * 4,
        out_shape=[like, like, like, jax.ShapeDtypeStruct(master.shape, BF16)],
        name="gu_adam",
    )(grads, master, first, second, codes, expo)


def down_update(grads, master, first, second, codes, expo):
    rows, cols = master.shape
    size = rows // 2
    block = pl.BlockSpec((size, cols), lambda i: (i, 0))
    narrow = pl.BlockSpec((size // 4, cols), lambda i: (i, 0))
    whole = pl.BlockSpec((1, cols), lambda i: (0, 0))
    like = jax.ShapeDtypeStruct(master.shape, F32)
    return pl.pallas_call(
        down_adam_kernel,
        grid=(2,),
        in_specs=[
            pl.BlockSpec((1, cols, size), lambda i: (2, 0, i)),
            block,
            block,
            block,
            narrow,
            whole,
        ],
        out_specs=[block] * 4,
        out_shape=[like, like, like, jax.ShapeDtypeStruct(master.shape, BF16)],
        name="down_adam",
    )(grads, master, first, second, codes, expo)


def piece_rows(pieces, ring, lo_step, side):
    own, other = pieces
    if ring < 3:
        return jnp.concatenate([own[ring][lo_step, side], other[ring][lo_step, side]], axis=1)
    half, at = lo_step // 2, lo_step % 2
    return jnp.concatenate(
        [own[3 + half][at, side], other[3 + half][at, side]], axis=1
    )


def weight_rows(weights, block, which, low, core):
    start = pl.multiple_of(low * 256 + core * 128, 128)
    second = pl.multiple_of(low * 256 + (1 - core) * 128, 128)
    return jnp.concatenate(
        [weights[block, which, pl.ds(start, 128), :], weights[block, which, pl.ds(second, 128), :]],
        axis=0,
    )


def partial_kernel(mine, place, *refs):
    own, other, weights, out = refs[:5], refs[5:10], refs[10], refs[11]
    acc = refs[12]
    hi, lo, y, core = place[1], place[2], place[3], place[4]
    target = hi if mine else 1 - hi
    acc[...] = jnp.zeros_like(acc)
    for ring, offset in enumerate(Y_OFFSETS):
        from_y = (y + offset) & 3

        @pl.when((from_y >> 1) == target)
        def _():
            for lo_step in range(4):
                block = (lo - lo_step) & 3
                for which in range(3):
                    left = piece_rows((own, other), ring, lo_step, which // 2)
                    right = weight_rows(weights, block, which, from_y & 1, core)
                    acc[which] += jnp.dot(left, right, preferred_element_type=F32)

    out[...] = acc[...].astype(out.dtype)


def partial(mine, place, pieces, weights):
    return pl.pallas_call(
        lambda *refs: partial_kernel(mine, *refs),
        in_specs=[SMEM] + [VMEM] * 11,
        out_specs=VMEM,
        out_shape=jax.ShapeDtypeStruct((3, 256, 256), F32 if mine else BF16),
        scratch_shapes=[pltpu.VMEM((3, 256, 256), F32)],
        compiler_params=pltpu.CompilerParams(vmem_limit_bytes=40 * 2**20),
        name="partial_own" if mine else "partial_sent",
    )(place, *pieces, weights)


def gated_kernel(own, sent, out):
    gate = own[0] + sent[0].astype(F32)
    up = own[1] + sent[1].astype(F32)
    dh = own[2] + sent[2].astype(F32)
    sig = jax.nn.sigmoid(gate)
    act = gate * sig
    out[0] = (dh * up * sig * (1.0 + gate * (1.0 - sig))).astype(BF16)
    out[1] = (dh * act).astype(BF16)
    out[2] = (act * up).astype(BF16)


def gated(own, sent):
    return pl.pallas_call(
        gated_kernel,
        in_specs=[VMEM] * 2,
        out_specs=VMEM,
        out_shape=jax.ShapeDtypeStruct((3, 256, 256), BF16),
        name="gated",
    )(own, sent)


def cross(left, right, left_dim, right_dim):
    return lax.dot_general(
        left, right, (((left_dim,), (right_dim,)), ((), ())), preferred_element_type=F32
    )


def outputs_kernel(mine, place, rows_own, rows_other, weights, out):
    hi, lo, y, core = place[1], place[2], place[3], place[4]
    core = core if mine else 1 - core
    for ring in range(4):
        to_y = (y + ring) & 3
        start = pl.multiple_of((to_y & 1) * 256 + core * 128, 128)

        def fill(rows):
            for lo_step in range(4):
                block = (lo + lo_step) & 3
                parts = [weights[block, which, pl.ds(start, 128), :] for which in range(3)]
                out[ring, lo_step, 0] = cross(rows[2], parts[2], 1, 1).astype(out.dtype)
                out[ring, lo_step, 1] = (
                    cross(rows[0], parts[0], 1, 1) + cross(rows[1], parts[1], 1, 1)
                ).astype(out.dtype)

        @pl.when((to_y >> 1) == hi)
        def _():
            fill(rows_own)

        @pl.when((to_y >> 1) != hi)
        def _():
            fill(rows_other)


def outputs(mine, place, rows_own, rows_other, weights):
    return pl.pallas_call(
        lambda *refs: outputs_kernel(mine, *refs),
        in_specs=[SMEM] + [VMEM] * 3,
        out_specs=VMEM,
        out_shape=jax.ShapeDtypeStruct((4, 4, 2, 256, 128), BF16),
        compiler_params=pltpu.CompilerParams(vmem_limit_bytes=40 * 2**20),
        name="outputs_kept" if mine else "outputs_sent",
    )(place, rows_own, rows_other, weights)


def grads_kernel(inverse_scale, place, *refs):
    own, other, rows_own, rows_other, out, acc = refs[:5], refs[5:10], refs[10], refs[11], refs[12], refs[13]
    hi, lo, y, core = place[1], place[2], place[3], place[4]
    for ring, offset in enumerate(Y_OFFSETS):
        from_y = (y + offset) & 3
        low = from_y & 1

        def add(rows):
            for lo_step in range(4):
                block = (lo - lo_step) & 3
                for which in range(3):
                    left = piece_rows((own, other), ring, lo_step, which // 2)
                    term = cross(left, rows[which], 0, 0)
                    start = pl.multiple_of(low * 256 + core * 128, 128)
                    second = pl.multiple_of(low * 256 + (1 - core) * 128, 128)
                    acc[block, which, pl.ds(start, 128), :] += term[:128]
                    acc[block, which, pl.ds(second, 128), :] += term[128:]

        if ring == 0:
            acc[...] = jnp.zeros_like(acc)

        @pl.when((from_y >> 1) == hi)
        def _():
            add(rows_own)

        @pl.when((from_y >> 1) != hi)
        def _():
            add(rows_other)

    out[...] = (acc[...] * inverse_scale).astype(out.dtype)


def grads(inverse_scale, place, pieces, rows_own, rows_other):
    return pl.pallas_call(
        lambda *refs: grads_kernel(inverse_scale, *refs),
        in_specs=[SMEM] + [VMEM] * 12,
        out_specs=VMEM,
        out_shape=jax.ShapeDtypeStruct((4, 3, 512, 256), BF16),
        scratch_shapes=[pltpu.VMEM((4, 3, 512, 256), F32)],
        compiler_params=pltpu.CompilerParams(vmem_limit_bytes=48 * 2**20),
        name="grads",
    )(place, *pieces, rows_own, rows_other)


def gather_pieces(tokens, cotangent):
    start = move(jnp.stack([tokens, cotangent]), swap_hi_y)
    line = jnp.stack([start] + [move(start, along_lo(step)) for step in (1, 2, 3)])
    before = move(line, along_y(1))
    after = move(line, along_y(-1))
    far_low = move(before[:2], along_y(1))
    far_high = move(after[2:], along_y(-1))
    own = (line, before, after, far_low, far_high)
    return own + tuple(move(piece, other_core) for piece in own)


def scatter_outputs(kept, sent):
    f32 = lambda value: value.astype(F32)
    arrived = move(sent, other_core)
    total = (f32(kept) + f32(arrived)).astype(BF16)
    low = move(total[2, :2], along_y(1))
    high = move(total[2, 2:], along_y(-1))
    ahead = jnp.concatenate([(f32(total[1, :2]) + f32(low)).astype(BF16), total[1, 2:]])
    behind = jnp.concatenate([total[3, :2], (f32(total[3, 2:]) + f32(high)).astype(BF16)])
    from_before = move(ahead, along_y(1))
    from_after = move(behind, along_y(-1))
    line = f32(total[0]) + f32(from_before) + f32(from_after)
    leaving = line[1:].astype(BF16)
    result = line[0]
    for step in (1, 2, 3):
        result = result + f32(move(leaving[step - 1], along_lo(step)))
    return move(result.astype(BF16), swap_hi_y)


def shards(
    tokens,
    cotangent,
    gu_master,
    gu_first,
    gu_second,
    gu_codes,
    gu_expo,
    down_master,
    down_first,
    down_second,
    down_codes,
    down_expo,
):
    dp, tensor = lax.axis_index("dp"), lax.axis_index("tensor")
    place = jnp.stack([dp >> 1, dp & 1, tensor >> 3, (tensor >> 1) & 3, tensor & 1])
    down_expo = down_expo.reshape(1, -1)
    quant = pl.pallas_call(
        quantize_kernel,
        in_specs=[VMEM] * 6,
        out_specs=VMEM,
        out_shape=jax.ShapeDtypeStruct((3, 512, 256), BF16),
        name="quantize",
    )(gu_master, gu_codes, gu_expo, down_master, down_codes, down_expo)
    weights = lax.all_gather(
        quant.reshape(1536, 256), "dp", axis=0, tiled=True, axis_index_groups=X_GROUPS
    ).reshape(4, 3, 512, 256)
    pieces = gather_pieces(tokens, cotangent)
    sent = partial(False, place, pieces, weights)
    arrived = move(sent, other_hi)
    kept = partial(True, place, pieces, weights)
    rows_own = gated(kept, arrived)
    rows_other = move(rows_own, other_hi)
    out_sent = outputs(False, place, rows_own, rows_other, weights)
    out_kept = outputs(True, place, rows_own, rows_other, weights)
    inverse_scale = 1.0 / (tokens.shape[0] * lax.axis_size("dp"))
    grad = grads(inverse_scale, place, pieces, rows_own, rows_other)
    grad = lax.psum_scatter(
        grad.reshape(6144, 256), "dp", scatter_dimension=0, tiled=True, axis_index_groups=X_GROUPS
    ).reshape(3, 512, 256)
    both = scatter_outputs(out_kept, out_sent)
    gu_new, gu_first_new, gu_second_new, gu_copy = gu_update(
        grad, gu_master, gu_first, gu_second, gu_codes, gu_expo
    )
    down_new, down_first_new, down_second_new, down_copy = down_update(
        grad, down_master, down_first, down_second, down_codes, down_expo
    )
    return (
        both[0],
        both[1],
        gu_new,
        gu_first_new,
        gu_second_new,
        gu_copy,
        down_new,
        down_first_new,
        down_second_new,
        down_copy,
    )


def solution(mesh):
    in_specs = (
        P("dp", "tensor"),
        P("dp", "tensor"),
        P(None, "dp", "tensor"),
        P(None, "dp", "tensor"),
        P(None, "dp", "tensor"),
        P(None, "dp", "tensor"),
        P(None, "tensor"),
        P("tensor", "dp"),
        P("tensor", "dp"),
        P("tensor", "dp"),
        P("tensor", "dp"),
        P("dp"),
    )
    out_specs = (
        P("dp", "tensor"),
        P("dp", "tensor"),
        P(None, "dp", "tensor"),
        P(None, "dp", "tensor"),
        P(None, "dp", "tensor"),
        P(None, "dp", "tensor"),
        P("tensor", "dp"),
        P("tensor", "dp"),
        P("tensor", "dp"),
        P("tensor", "dp"),
    )
    return jax.shard_map(shards, mesh=mesh, in_specs=in_specs, out_specs=out_specs, check_vma=False)
```

```python
import jax
import jax.numpy as jnp
from jax import lax
from jax.experimental import pallas as pl
from jax.experimental.pallas import tpu as pltpu
from jax.sharding import PartitionSpec as P

BETA_ONE = 0.9
BETA_TWO = 0.95
ADAM_EPS = 1e-08
LEARN_RATE = 0.002
CORRECT_ONE = 1.0 - 0.9**10
CORRECT_TWO = 1.0 - 0.95**10

ALL = ("dp", "tensor")
F32 = jnp.float32
BF16 = jnp.bfloat16
VMEM = pl.BlockSpec(memory_space=pltpu.VMEM)
SMEM = pl.BlockSpec(memory_space=pltpu.SMEM)
X_GROUPS = [[hi + 2 * x for x in range(4)] for hi in range(2)]
Y_OFFSETS = (0, 3, 1, 2)


def limit(mebibytes):
    return pltpu.CompilerParams(vmem_limit_bytes=mebibytes * 2**20)


def device_number(x, hi, lo, y, core):
    return (x * 2 + hi) * 32 + lo * 8 + y * 2 + core


def move(value, target):
    pairs = []
    for x in range(4):
        for hi in range(2):
            for lo in range(4):
                for y in range(4):
                    for core in range(2):
                        here = device_number(x, hi, lo, y, core)
                        pairs.append((here, device_number(*target(x, hi, lo, y, core))))
    return lax.ppermute(value, ALL, pairs)


def after(value, *others):
    return lax.optimization_barrier((value, *others))[0]


def along_y(step):
    return lambda x, hi, lo, y, core: (x, hi, lo, (y + step) % 4, core)


def along_lo(step):
    return lambda x, hi, lo, y, core: (x, hi, (lo + step) % 4, y, core)


def other_hi(x, hi, lo, y, core):
    return (x, 1 - hi, lo, y, core)


def other_core(x, hi, lo, y, core):
    return (x, hi, lo, y, 1 - core)


def swap_hi_y(x, hi, lo, y, core):
    return (x, y >> 1, lo, hi * 2 + (y & 1), core)


def power_of_two(expo, sign):
    result = jnp.zeros(expo.shape, F32)
    for level in range(-8, 0):
        result = jnp.where(expo == level, jnp.float32(2.0 ** (sign * level)), result)
    return result


def expand_codes(codes):
    groups = codes.shape[0]
    rows = groups * 4
    spread = (
        (lax.broadcasted_iota(jnp.int32, (rows, groups), 0) >> 2)
        == lax.broadcasted_iota(jnp.int32, (rows, groups), 1)
    ).astype(F32).astype(BF16)
    code = jnp.dot(spread, codes.astype(F32).astype(BF16), preferred_element_type=F32)
    place = (lax.broadcasted_iota(jnp.int32, code.shape, 0) & 3).astype(F32)
    first = jnp.where(code < 2.5, 0.0, jnp.where(code < 4.5, 1.0, 2.0))
    second = jnp.where(
        code == 0.0, 1.0, jnp.where((code == 1.0) | (code == 3.0), 2.0, 3.0)
    )
    return ((place == first) | (place == second)).astype(F32)


def quantize(master, keeper, scale, inverse):
    inner = jnp.clip(master * inverse, -1.0, 1.0) * keeper
    return inner.astype(BF16) * scale.astype(BF16)


def quantize_kernel(gu_ref, gu_codes, gu_expo, dn_ref, dn_codes, dn_expo, out_ref):
    for part in range(2):
        expo = gu_expo[part : part + 1, :]
        out_ref[part] = quantize(
            gu_ref[part],
            expand_codes(gu_codes[part]),
            power_of_two(expo, 1),
            power_of_two(expo, -1),
        )
    expo = dn_expo[...]
    down = jnp.clip(dn_ref[...] * power_of_two(expo, -1), -1.0, 1.0) * expand_codes(dn_codes[...])
    down = down.astype(BF16) * power_of_two(expo, 1).astype(BF16)
    out_ref[2] = down.astype(F32).T.astype(BF16)


def adam(master, first, second, grad, codes, expo):
    keeper = expand_codes(codes)
    inverse = power_of_two(expo, -1)
    inside = (jnp.abs(master * inverse) <= 1.0).astype(F32)
    grad = grad * keeper * inside
    first = BETA_ONE * first + (1.0 - BETA_ONE) * grad
    second = BETA_TWO * second + (1.0 - BETA_TWO) * grad * grad
    step = (LEARN_RATE / CORRECT_ONE) * first
    master = master - step / (jnp.sqrt(second * (1.0 / CORRECT_TWO)) + ADAM_EPS)
    return master, first, second, quantize(master, keeper, power_of_two(expo, 1), inverse)


def gu_adam_kernel(grad, master, first, second, codes, expo, new, new_first, new_second, copy):
    which = pl.program_id(0)
    chosen = jnp.where(which == 0, expo[0:1, :], expo[1:2, :])
    result = adam(
        master[0], first[0], second[0], grad[0].astype(F32), codes[0], chosen
    )
    new[0], new_first[0], new_second[0], copy[0] = result


def down_adam_kernel(grad, master, first, second, codes, expo, new, new_first, new_second, copy):
    result = adam(
        master[...], first[...], second[...], grad[0].astype(F32).T, codes[...], expo[...]
    )
    new[...], new_first[...], new_second[...], copy[...] = result


def gu_update(grads, master, first, second, codes, expo):
    parts, rows, cols = master.shape
    size = rows // 2
    block = pl.BlockSpec((1, size, cols), lambda i, j: (i, j, 0))
    narrow = pl.BlockSpec((1, size // 4, cols), lambda i, j: (i, j, 0))
    whole = pl.BlockSpec((parts, cols), lambda i, j: (0, 0))
    like = jax.ShapeDtypeStruct(master.shape, F32)
    return pl.pallas_call(
        gu_adam_kernel,
        grid=(parts, 2),
        in_specs=[block, block, block, block, narrow, whole],
        out_specs=[block] * 4,
        out_shape=[like, like, like, jax.ShapeDtypeStruct(master.shape, BF16)],
        name="gu_adam",
    )(grads, master, first, second, codes, expo)


def down_update(grads, master, first, second, codes, expo):
    rows, cols = master.shape
    size = rows // 2
    block = pl.BlockSpec((size, cols), lambda i: (i, 0))
    narrow = pl.BlockSpec((size // 4, cols), lambda i: (i, 0))
    whole = pl.BlockSpec((1, cols), lambda i: (0, 0))
    like = jax.ShapeDtypeStruct(master.shape, F32)
    return pl.pallas_call(
        down_adam_kernel,
        grid=(2,),
        in_specs=[
            pl.BlockSpec((1, cols, size), lambda i: (2, 0, i)),
            block,
            block,
            block,
            narrow,
            whole,
        ],
        out_specs=[block] * 4,
        out_shape=[like, like, like, jax.ShapeDtypeStruct(master.shape, BF16)],
        name="down_adam",
    )(grads, master, first, second, codes, expo)


def piece_rows(pieces, ring, lo_step, side):
    own, other = pieces
    if ring < 3:
        return jnp.concatenate([own[ring][lo_step, side], other[ring][lo_step, side]], axis=1)
    half, at = lo_step // 2, lo_step % 2
    return jnp.concatenate(
        [own[3 + half][at, side], other[3 + half][at, side]], axis=1
    )


def weight_rows(weights, block, which, low, core):
    start = pl.multiple_of(low * 256 + core * 128, 128)
    second = pl.multiple_of(low * 256 + (1 - core) * 128, 128)
    return jnp.concatenate(
        [weights[block, which, pl.ds(start, 128), :], weights[block, which, pl.ds(second, 128), :]],
        axis=0,
    )


def partial_kernel(mine, place, *refs):
    own, other, weights, out = refs[:5], refs[5:10], refs[10], refs[11]
    acc = refs[12]
    hi, lo, y, core = place[1], place[2], place[3], place[4]
    target = hi if mine else 1 - hi
    acc[...] = jnp.zeros_like(acc)
    for ring, offset in enumerate(Y_OFFSETS):
        from_y = (y + offset) & 3

        @pl.when((from_y >> 1) == target)
        def _():
            for lo_step in range(4):
                block = (lo - lo_step) & 3
                for which in range(3):
                    left = piece_rows((own, other), ring, lo_step, which // 2)
                    right = weight_rows(weights, block, which, from_y & 1, core)
                    acc[which] += jnp.dot(left, right, preferred_element_type=F32)

    out[...] = acc[...].astype(out.dtype)


def partial(mine, place, pieces, weights):
    return pl.pallas_call(
        lambda *refs: partial_kernel(mine, *refs),
        in_specs=[SMEM] + [VMEM] * 11,
        out_specs=VMEM,
        out_shape=jax.ShapeDtypeStruct((3, 256, 256), F32 if mine else BF16),
        scratch_shapes=[pltpu.VMEM((3, 256, 256), F32)],
        compiler_params=limit(16),
        name="partial_own" if mine else "partial_sent",
    )(place, *pieces, weights)


def gated_kernel(own, sent, out):
    gate = own[0] + sent[0].astype(F32)
    up = own[1] + sent[1].astype(F32)
    dh = own[2] + sent[2].astype(F32)
    sig = jax.nn.sigmoid(gate)
    act = gate * sig
    out[0] = (dh * up * sig * (1.0 + gate * (1.0 - sig))).astype(BF16)
    out[1] = (dh * act).astype(BF16)
    out[2] = (act * up).astype(BF16)


def gated(own, sent):
    return pl.pallas_call(
        gated_kernel,
        in_specs=[VMEM] * 2,
        out_specs=VMEM,
        out_shape=jax.ShapeDtypeStruct((3, 256, 256), BF16),
        name="gated",
    )(own, sent)


def cross(left, right, left_dim, right_dim):
    return lax.dot_general(
        left, right, (((left_dim,), (right_dim,)), ((), ())), preferred_element_type=F32
    )


def outputs_kernel(sides, place, rows, weights, *outs):
    lo, core = place[2], place[4]
    for side, out in zip(sides, outs):
        to_core = core if side == "kept" else 1 - core
        for low in range(2):
            start = pl.multiple_of(low * 256 + to_core * 128, 128)
            for lo_step in range(4):
                block = (lo + lo_step) & 3
                parts = [weights[block, which, pl.ds(start, 128), :] for which in range(3)]
                out[low, lo_step, 0] = cross(rows[2], parts[2], 1, 1).astype(out.dtype)
                out[low, lo_step, 1] = (
                    cross(rows[0], parts[0], 1, 1) + cross(rows[1], parts[1], 1, 1)
                ).astype(out.dtype)


def outputs(sides, place, rows, weights):
    return pl.pallas_call(
        lambda *refs: outputs_kernel(sides, *refs),
        in_specs=[SMEM] + [VMEM] * 2,
        out_specs=[VMEM] * len(sides),
        out_shape=[jax.ShapeDtypeStruct((2, 4, 2, 256, 128), BF16)] * len(sides),
        compiler_params=limit(16),
        name="outputs_" + "_".join(sides),
    )(place, rows, weights)


def combine_kernel(place, own_kept, own_got, arrived_kept, arrived_got, out):
    hi, y = place[1], place[3]
    for step in range(4):
        to_y = (y + step) & 3
        low = to_y & 1

        @pl.when((to_y >> 1) == hi)
        def _():
            out[step] = (own_kept[low].astype(F32) + own_got[low].astype(F32)).astype(BF16)

        @pl.when((to_y >> 1) != hi)
        def _():
            out[step] = (arrived_kept[low].astype(F32) + arrived_got[low].astype(F32)).astype(BF16)


def combine(place, *halves):
    return pl.pallas_call(
        combine_kernel,
        in_specs=[SMEM] + [VMEM] * 4,
        out_specs=VMEM,
        out_shape=jax.ShapeDtypeStruct((4, 4, 2, 256, 128), BF16),
        compiler_params=limit(16),
        name="combine",
    )(place, *halves)


def grads_kernel(own_rows, inverse_scale, place, *refs):
    own, other, rows, out = refs[:5], refs[5:10], refs[10], refs[-1]
    hi, lo, y, core = place[1], place[2], place[3], place[4]
    target = hi if own_rows else 1 - hi
    for ring, offset in enumerate(Y_OFFSETS):
        from_y = (y + offset) & 3

        @pl.when((from_y >> 1) == target)
        def _():
            low = from_y & 1
            first = pl.ds(pl.multiple_of(low * 256 + core * 128, 128), 128)
            second = pl.ds(pl.multiple_of(low * 256 + (1 - core) * 128, 128), 128)
            for lo_step in range(4):
                block = (lo - lo_step) & 3
                for which in range(3):
                    left = piece_rows((own, other), ring, lo_step, which // 2)
                    term = cross(left, rows[which], 0, 0) * inverse_scale
                    upper, lower = term[:128], term[128:]
                    if not own_rows:
                        before = refs[11]
                        upper += before[block, which, first, :].astype(F32)
                        lower += before[block, which, second, :].astype(F32)
                    out[block, which, first, :] = upper.astype(BF16)
                    out[block, which, second, :] = lower.astype(BF16)


def grads(own_rows, inverse_scale, place, pieces, rows, *before):
    return pl.pallas_call(
        lambda *refs: grads_kernel(own_rows, inverse_scale, *refs),
        in_specs=[SMEM] + [VMEM] * (11 + len(before)),
        out_specs=VMEM,
        out_shape=jax.ShapeDtypeStruct((4, 3, 512, 256), BF16),
        compiler_params=limit(24),
        name="own_grads" if own_rows else "arrived_grads",
    )(place, *pieces, rows, *before)


def gather_pieces(tokens, cotangent):
    start = move(jnp.stack([tokens, cotangent]), swap_hi_y)
    line = jnp.stack([start] + [move(start, along_lo(step)) for step in (1, 2, 3)])
    before = move(line, along_y(1))
    after = move(line, along_y(-1))
    far_low = move(before[:2], along_y(1))
    far_high = move(after[2:], along_y(-1))
    own = (line, before, after, far_low, far_high)
    return own + tuple(move(piece, other_core) for piece in own)


def scatter_outputs(total):
    f32 = lambda value: value.astype(F32)
    low = move(total[2, :2], along_y(1))
    high = move(total[2, 2:], along_y(-1))
    ahead = jnp.concatenate([(f32(total[1, :2]) + f32(low)).astype(BF16), total[1, 2:]])
    behind = jnp.concatenate([total[3, :2], (f32(total[3, 2:]) + f32(high)).astype(BF16)])
    from_before = move(ahead, along_y(1))
    from_after = move(behind, along_y(-1))
    line = f32(total[0]) + f32(from_before) + f32(from_after)
    leaving = line[1:].astype(BF16)
    result = line[0]
    for step in (1, 2, 3):
        result = result + f32(move(leaving[step - 1], along_lo(step)))
    return result.astype(BF16)


def shards(
    tokens,
    cotangent,
    gu_master,
    gu_first,
    gu_second,
    gu_codes,
    gu_expo,
    down_master,
    down_first,
    down_second,
    down_codes,
    down_expo,
):
    dp, tensor = lax.axis_index("dp"), lax.axis_index("tensor")
    place = jnp.stack([dp >> 1, dp & 1, tensor >> 3, (tensor >> 1) & 3, tensor & 1])
    down_expo = down_expo.reshape(1, -1)
    quant = pl.pallas_call(
        quantize_kernel,
        in_specs=[VMEM] * 6,
        out_specs=VMEM,
        out_shape=jax.ShapeDtypeStruct((3, 512, 256), BF16),
        name="quantize",
    )(gu_master, gu_codes, gu_expo, down_master, down_codes, down_expo)
    weights = lax.all_gather(
        quant.reshape(1536, 256), "dp", axis=0, tiled=True, axis_index_groups=X_GROUPS
    ).reshape(4, 3, 512, 256)
    pieces = gather_pieces(tokens, cotangent)
    sent = partial(False, place, pieces, weights)
    arrived = move(sent, other_hi)
    kept = partial(True, place, pieces, weights)
    rows_own = gated(kept, arrived)
    rows_other = move(rows_own, other_hi)
    inverse_scale = 1.0 / (tokens.shape[0] * lax.axis_size("dp"))
    grad = grads(True, inverse_scale, place, pieces, rows_own)
    rows_own, grad = lax.optimization_barrier((rows_own, grad))
    own_sent, own_kept = outputs(("sent", "kept"), place, rows_own, weights)
    own_got = move(own_sent, other_core)
    rows_other, own_kept = lax.optimization_barrier((rows_other, own_kept))
    grad = grads(False, inverse_scale, place, pieces, rows_other, grad)
    grad = lax.psum_scatter(
        grad.reshape(6144, 256), "dp", scatter_dimension=0, tiled=True, axis_index_groups=X_GROUPS
    ).reshape(3, 512, 256)
    (sent,) = outputs(("sent",), place, rows_other, weights)
    got = move(sent, other_core)
    (kept,) = outputs(("kept",), place, rows_other, weights)
    both = scatter_outputs(combine(place, own_kept, own_got, kept, got))
    gu_new, gu_first_new, gu_second_new, gu_copy = gu_update(
        grad, gu_master, gu_first, gu_second, gu_codes, gu_expo
    )
    down_new, down_first_new, down_second_new, down_copy = down_update(
        grad, down_master, down_first, down_second, down_codes, down_expo
    )
    both = after(move(both, swap_hi_y), gu_copy, down_copy)
    return (
        both[0],
        both[1],
        gu_new,
        gu_first_new,
        gu_second_new,
        gu_copy,
        down_new,
        down_first_new,
        down_second_new,
        down_copy,
    )


def solution(mesh):
    in_specs = (
        P("dp", "tensor"),
        P("dp", "tensor"),
        P(None, "dp", "tensor"),
        P(None, "dp", "tensor"),
        P(None, "dp", "tensor"),
        P(None, "dp", "tensor"),
        P(None, "tensor"),
        P("tensor", "dp"),
        P("tensor", "dp"),
        P("tensor", "dp"),
        P("tensor", "dp"),
        P("dp"),
    )
    out_specs = (
        P("dp", "tensor"),
        P("dp", "tensor"),
        P(None, "dp", "tensor"),
        P(None, "dp", "tensor"),
        P(None, "dp", "tensor"),
        P(None, "dp", "tensor"),
        P("tensor", "dp"),
        P("tensor", "dp"),
        P("tensor", "dp"),
        P("tensor", "dp"),
    )
    return jax.shard_map(shards, mesh=mesh, in_specs=in_specs, out_specs=out_specs, check_vma=False)
```

```python
import jax
import jax.numpy as jnp
from jax import lax
from jax.experimental import pallas as pl
from jax.experimental.pallas import tpu as pltpu
from jax.sharding import PartitionSpec as P

BETA_ONE = 0.9
BETA_TWO = 0.95
ADAM_EPS = 1e-08
LEARN_RATE = 0.002
CORRECT_ONE = 1.0 - 0.9**10
CORRECT_TWO = 1.0 - 0.95**10

ALL = ("dp", "tensor")
F32 = jnp.float32
BF16 = jnp.bfloat16
VMEM = pl.BlockSpec(memory_space=pltpu.VMEM)
SMEM = pl.BlockSpec(memory_space=pltpu.SMEM)
X_GROUPS = [[hi + 2 * x for x in range(4)] for hi in range(2)]
Y_OFFSETS = (0, 3, 1, 2)


def limit(mebibytes):
    return pltpu.CompilerParams(vmem_limit_bytes=mebibytes * 2**20)


def device_number(x, hi, lo, y, core):
    return (x * 2 + hi) * 32 + lo * 8 + y * 2 + core


def move(value, target):
    pairs = []
    for x in range(4):
        for hi in range(2):
            for lo in range(4):
                for y in range(4):
                    for core in range(2):
                        here = device_number(x, hi, lo, y, core)
                        pairs.append((here, device_number(*target(x, hi, lo, y, core))))
    return lax.ppermute(value, ALL, pairs)


def after(value, *others):
    return lax.optimization_barrier((value, *others))[0]


def along_y(step):
    return lambda x, hi, lo, y, core: (x, hi, lo, (y + step) % 4, core)


def along_lo(step):
    return lambda x, hi, lo, y, core: (x, hi, (lo + step) % 4, y, core)


def other_hi(x, hi, lo, y, core):
    return (x, 1 - hi, lo, y, core)


def other_core(x, hi, lo, y, core):
    return (x, hi, lo, y, 1 - core)


def to_half(x, hi, lo, y, core):
    if hi != y >> 1:
        return (x, 1 - hi, lo, y, core)
    return (x, hi, lo, y ^ 2, core)


def from_half(x, hi, lo, y, core):
    if hi != y >> 1:
        return (x, hi, lo, y ^ 2, core)
    return (x, 1 - hi, lo, y, core)


def power_of_two(expo, sign):
    result = jnp.zeros(expo.shape, F32)
    for level in range(-8, 0):
        result = jnp.where(expo == level, jnp.float32(2.0 ** (sign * level)), result)
    return result


def expand_codes(codes):
    groups = codes.shape[0]
    rows = groups * 4
    spread = (
        (lax.broadcasted_iota(jnp.int32, (rows, groups), 0) >> 2)
        == lax.broadcasted_iota(jnp.int32, (rows, groups), 1)
    ).astype(F32).astype(BF16)
    code = jnp.dot(spread, codes.astype(F32).astype(BF16), preferred_element_type=F32)
    place = (lax.broadcasted_iota(jnp.int32, code.shape, 0) & 3).astype(F32)
    first = jnp.where(code < 2.5, 0.0, jnp.where(code < 4.5, 1.0, 2.0))
    second = jnp.where(
        code == 0.0, 1.0, jnp.where((code == 1.0) | (code == 3.0), 2.0, 3.0)
    )
    return ((place == first) | (place == second)).astype(F32)


def quantize(master, keeper, scale, inverse):
    inner = jnp.clip(master * inverse, -1.0, 1.0) * keeper
    return inner.astype(BF16) * scale.astype(BF16)


def quantize_kernel(gu_ref, gu_codes, gu_expo, dn_ref, dn_codes, dn_expo, out_ref):
    for part in range(2):
        expo = gu_expo[part : part + 1, :]
        out_ref[part] = quantize(
            gu_ref[part],
            expand_codes(gu_codes[part]),
            power_of_two(expo, 1),
            power_of_two(expo, -1),
        )
    expo = dn_expo[...]
    down = jnp.clip(dn_ref[...] * power_of_two(expo, -1), -1.0, 1.0) * expand_codes(dn_codes[...])
    down = down.astype(BF16) * power_of_two(expo, 1).astype(BF16)
    out_ref[2] = down.astype(F32).T.astype(BF16)


def adam(master, first, second, grad, codes, expo):
    keeper = expand_codes(codes)
    inverse = power_of_two(expo, -1)
    inside = (jnp.abs(master * inverse) <= 1.0).astype(F32)
    grad = grad * keeper * inside
    first = BETA_ONE * first + (1.0 - BETA_ONE) * grad
    second = BETA_TWO * second + (1.0 - BETA_TWO) * grad * grad
    step = (LEARN_RATE / CORRECT_ONE) * first
    master = master - step / (jnp.sqrt(second * (1.0 / CORRECT_TWO)) + ADAM_EPS)
    return master, first, second, quantize(master, keeper, power_of_two(expo, 1), inverse)


def gu_adam_kernel(grad, master, first, second, codes, expo, new, new_first, new_second, copy):
    which = pl.program_id(0)
    chosen = jnp.where(which == 0, expo[0:1, :], expo[1:2, :])
    result = adam(
        master[0], first[0], second[0], grad[0].astype(F32), codes[0], chosen
    )
    new[0], new_first[0], new_second[0], copy[0] = result


def down_adam_kernel(grad, master, first, second, codes, expo, new, new_first, new_second, copy):
    result = adam(
        master[...], first[...], second[...], grad[0].astype(F32).T, codes[...], expo[...]
    )
    new[...], new_first[...], new_second[...], copy[...] = result


def gu_update(grads, master, first, second, codes, expo):
    parts, rows, cols = master.shape
    size = rows
    block = pl.BlockSpec((1, size, cols), lambda i, j: (i, j, 0))
    narrow = pl.BlockSpec((1, size // 4, cols), lambda i, j: (i, j, 0))
    whole = pl.BlockSpec((parts, cols), lambda i, j: (0, 0))
    like = jax.ShapeDtypeStruct(master.shape, F32)
    return pl.pallas_call(
        gu_adam_kernel,
        grid=(parts, 1),
        in_specs=[block, block, block, block, narrow, whole],
        out_specs=[block] * 4,
        out_shape=[like, like, like, jax.ShapeDtypeStruct(master.shape, BF16)],
        name="gu_adam",
    )(grads, master, first, second, codes, expo)


def down_update(grads, master, first, second, codes, expo):
    rows, cols = master.shape
    size = rows // 2
    block = pl.BlockSpec((size, cols), lambda i: (i, 0))
    narrow = pl.BlockSpec((size // 4, cols), lambda i: (i, 0))
    whole = pl.BlockSpec((1, cols), lambda i: (0, 0))
    like = jax.ShapeDtypeStruct(master.shape, F32)
    return pl.pallas_call(
        down_adam_kernel,
        grid=(2,),
        in_specs=[
            pl.BlockSpec((1, cols, size), lambda i: (2, 0, i)),
            block,
            block,
            block,
            narrow,
            whole,
        ],
        out_specs=[block] * 4,
        out_shape=[like, like, like, jax.ShapeDtypeStruct(master.shape, BF16)],
        name="down_adam",
    )(grads, master, first, second, codes, expo)


def piece_rows(pieces, ring, lo_step, side):
    own, other = pieces
    if ring < 3:
        return jnp.concatenate([own[ring][lo_step, side], other[ring][lo_step, side]], axis=1)
    half, at = lo_step // 2, lo_step % 2
    return jnp.concatenate(
        [own[3 + half][at, side], other[3 + half][at, side]], axis=1
    )


def weight_rows(weights, block, which, low, core):
    start = pl.multiple_of(low * 256 + core * 128, 128)
    second = pl.multiple_of(low * 256 + (1 - core) * 128, 128)
    return jnp.concatenate(
        [weights[block, which, pl.ds(start, 128), :], weights[block, which, pl.ds(second, 128), :]],
        axis=0,
    )


def partial_kernel(mine, place, *refs):
    own, other, weights, out = refs[:5], refs[5:10], refs[10], refs[11]
    acc = refs[12]
    hi, lo, y, core = place[1], place[2], place[3], place[4]
    target = 1 - hi if mine else hi
    acc[...] = jnp.zeros_like(acc)
    for ring, offset in enumerate(Y_OFFSETS):
        from_y = (y + offset) & 3

        @pl.when((from_y >> 1) == target)
        def _():
            for lo_step in range(4):
                block = (lo - lo_step) & 3
                for which in range(3):
                    left = piece_rows((own, other), ring, lo_step, which // 2)
                    right = weight_rows(weights, block, which, from_y & 1, core)
                    acc[which] += jnp.dot(left, right, preferred_element_type=F32)

    out[...] = acc[...].astype(out.dtype)


def partial(mine, place, pieces, weights):
    return pl.pallas_call(
        lambda *refs: partial_kernel(mine, *refs),
        in_specs=[SMEM] + [VMEM] * 11,
        out_specs=VMEM,
        out_shape=jax.ShapeDtypeStruct((3, 256, 256), F32 if mine else BF16),
        scratch_shapes=[pltpu.VMEM((3, 256, 256), F32)],
        compiler_params=limit(16),
        name="partial_own" if mine else "partial_sent",
    )(place, *pieces, weights)


def gated_kernel(own, sent, out):
    gate = own[0] + sent[0].astype(F32)
    up = own[1] + sent[1].astype(F32)
    dh = own[2] + sent[2].astype(F32)
    sig = jax.nn.sigmoid(gate)
    act = gate * sig
    out[0] = (dh * up * sig * (1.0 + gate * (1.0 - sig))).astype(BF16)
    out[1] = (dh * act).astype(BF16)
    out[2] = (act * up).astype(BF16)


def gated(own, sent):
    return pl.pallas_call(
        gated_kernel,
        in_specs=[VMEM] * 2,
        out_specs=VMEM,
        out_shape=jax.ShapeDtypeStruct((3, 256, 256), BF16),
        name="gated",
    )(own, sent)


def cross(left, right, left_dim, right_dim):
    return lax.dot_general(
        left, right, (((left_dim,), (right_dim,)), ((), ())), preferred_element_type=F32
    )


def outputs_kernel(sides, place, rows, weights, *outs):
    lo, core = place[2], place[4]
    for side, out in zip(sides, outs):
        to_core = core if side == "kept" else 1 - core
        for low in range(2):
            start = pl.multiple_of(low * 256 + to_core * 128, 128)
            for lo_step in range(4):
                block = (lo + lo_step) & 3
                parts = [weights[block, which, pl.ds(start, 128), :] for which in range(3)]
                out[low, lo_step, 0] = cross(rows[2], parts[2], 1, 1).astype(out.dtype)
                out[low, lo_step, 1] = (
                    cross(rows[0], parts[0], 1, 1) + cross(rows[1], parts[1], 1, 1)
                ).astype(out.dtype)


def outputs(sides, place, rows, weights):
    return pl.pallas_call(
        lambda *refs: outputs_kernel(sides, *refs),
        in_specs=[SMEM] + [VMEM] * 2,
        out_specs=[VMEM] * len(sides),
        out_shape=[jax.ShapeDtypeStruct((2, 4, 2, 256, 128), BF16)] * len(sides),
        compiler_params=limit(16),
        name="outputs_" + "_".join(sides),
    )(place, rows, weights)


def combine_kernel(place, own_kept, own_got, arrived_kept, arrived_got, out):
    hi, y = place[1], place[3]
    for step in range(4):
        to_y = (y + step) & 3
        low = to_y & 1

        @pl.when((to_y >> 1) != hi)
        def _():
            out[step] = (own_kept[low].astype(F32) + own_got[low].astype(F32)).astype(BF16)

        @pl.when((to_y >> 1) == hi)
        def _():
            out[step] = (arrived_kept[low].astype(F32) + arrived_got[low].astype(F32)).astype(BF16)


def combine(place, *halves):
    return pl.pallas_call(
        combine_kernel,
        in_specs=[SMEM] + [VMEM] * 4,
        out_specs=VMEM,
        out_shape=jax.ShapeDtypeStruct((4, 4, 2, 256, 128), BF16),
        compiler_params=limit(16),
        name="combine",
    )(place, *halves)


def grads_kernel(own_rows, inverse_scale, place, *refs):
    own, other, rows, out = refs[:5], refs[5:10], refs[10], refs[-1]
    hi, lo, y, core = place[1], place[2], place[3], place[4]
    target = 1 - hi if own_rows else hi
    for ring, offset in enumerate(Y_OFFSETS):
        from_y = (y + offset) & 3

        @pl.when((from_y >> 1) == target)
        def _():
            low = from_y & 1
            first = pl.ds(pl.multiple_of(low * 256 + core * 128, 128), 128)
            second = pl.ds(pl.multiple_of(low * 256 + (1 - core) * 128, 128), 128)
            for lo_step in range(4):
                block = (lo - lo_step) & 3
                for which in range(3):
                    left = piece_rows((own, other), ring, lo_step, which // 2)
                    term = cross(left, rows[which], 0, 0) * inverse_scale
                    upper, lower = term[:128], term[128:]
                    if not own_rows:
                        before = refs[11]
                        upper += before[block, which, first, :].astype(F32)
                        lower += before[block, which, second, :].astype(F32)
                    out[block, which, first, :] = upper.astype(BF16)
                    out[block, which, second, :] = lower.astype(BF16)


def grads(own_rows, inverse_scale, place, pieces, rows, *before):
    return pl.pallas_call(
        lambda *refs: grads_kernel(own_rows, inverse_scale, *refs),
        in_specs=[SMEM] + [VMEM] * (11 + len(before)),
        out_specs=VMEM,
        out_shape=jax.ShapeDtypeStruct((4, 3, 512, 256), BF16),
        compiler_params=limit(24),
        name="own_grads" if own_rows else "arrived_grads",
    )(place, *pieces, rows, *before)


def gather_pieces(tokens, cotangent, weights):
    start = move(jnp.stack([tokens, cotangent]), to_half)
    line = jnp.stack([start] + [move(start, along_lo(step)) for step in (1, 2, 3)])
    before = move(line, along_y(1))
    after = move(line, along_y(-1))
    far_low = move(before[:2], along_y(1))
    far_high = move(after[2:], along_y(-1))
    far_high, weights = lax.optimization_barrier((far_high, weights))
    own = (line, before, after, far_low, far_high)
    return own + tuple(move(piece, other_core) for piece in own), weights


def scatter_outputs(total):
    f32 = lambda value: value.astype(F32)
    low = move(total[2, :2], along_y(1))
    high = move(total[2, 2:], along_y(-1))
    ahead = jnp.concatenate([(f32(total[1, :2]) + f32(low)).astype(BF16), total[1, 2:]])
    behind = jnp.concatenate([total[3, :2], (f32(total[3, 2:]) + f32(high)).astype(BF16)])
    from_before = move(ahead, along_y(1))
    from_after = move(behind, along_y(-1))
    line = f32(total[0]) + f32(from_before) + f32(from_after)
    leaving = line[1:].astype(BF16)
    result = line[0]
    for step in (1, 2, 3):
        result = result + f32(move(leaving[step - 1], along_lo(step)))
    return result.astype(BF16)


def shards(
    tokens,
    cotangent,
    gu_master,
    gu_first,
    gu_second,
    gu_codes,
    gu_expo,
    down_master,
    down_first,
    down_second,
    down_codes,
    down_expo,
):
    dp, tensor = lax.axis_index("dp"), lax.axis_index("tensor")
    place = jnp.stack([dp >> 1, dp & 1, tensor >> 3, (tensor >> 1) & 3, tensor & 1])
    down_expo = down_expo.reshape(1, -1)
    quant = pl.pallas_call(
        quantize_kernel,
        in_specs=[VMEM] * 6,
        out_specs=VMEM,
        out_shape=jax.ShapeDtypeStruct((3, 512, 256), BF16),
        name="quantize",
    )(gu_master, gu_codes, gu_expo, down_master, down_codes, down_expo)
    weights = lax.all_gather(
        quant.reshape(1536, 256), "dp", axis=0, tiled=True, axis_index_groups=X_GROUPS
    ).reshape(4, 3, 512, 256)
    pieces, weights = gather_pieces(tokens, cotangent, weights)
    sent = partial(False, place, pieces, weights)
    arrived = move(sent, other_hi)
    kept = partial(True, place, pieces, weights)
    rows_own = gated(kept, arrived)
    rows_other = move(rows_own, other_hi)
    inverse_scale = 1.0 / (tokens.shape[0] * lax.axis_size("dp"))
    grad = grads(True, inverse_scale, place, pieces, rows_own)
    rows_own, grad = lax.optimization_barrier((rows_own, grad))
    own_sent, own_kept = outputs(("sent", "kept"), place, rows_own, weights)
    own_got = move(own_sent, other_core)
    rows_other, own_kept = lax.optimization_barrier((rows_other, own_kept))
    grad = grads(False, inverse_scale, place, pieces, rows_other, grad)
    grad = lax.psum_scatter(
        grad.reshape(6144, 256), "dp", scatter_dimension=0, tiled=True, axis_index_groups=X_GROUPS
    ).reshape(3, 512, 256)
    (sent,) = outputs(("sent",), place, rows_other, weights)
    got = move(sent, other_core)
    (kept,) = outputs(("kept",), place, rows_other, weights)
    both = scatter_outputs(combine(place, own_kept, own_got, kept, got))
    gu_new, gu_first_new, gu_second_new, gu_copy = gu_update(
        grad, gu_master, gu_first, gu_second, gu_codes, gu_expo
    )
    down_new, down_first_new, down_second_new, down_copy = down_update(
        grad, down_master, down_first, down_second, down_codes, down_expo
    )
    both = after(move(both, from_half), gu_copy, down_copy)
    return (
        both[0],
        both[1],
        gu_new,
        gu_first_new,
        gu_second_new,
        gu_copy,
        down_new,
        down_first_new,
        down_second_new,
        down_copy,
    )


def solution(mesh):
    in_specs = (
        P("dp", "tensor"),
        P("dp", "tensor"),
        P(None, "dp", "tensor"),
        P(None, "dp", "tensor"),
        P(None, "dp", "tensor"),
        P(None, "dp", "tensor"),
        P(None, "tensor"),
        P("tensor", "dp"),
        P("tensor", "dp"),
        P("tensor", "dp"),
        P("tensor", "dp"),
        P("dp"),
    )
    out_specs = (
        P("dp", "tensor"),
        P("dp", "tensor"),
        P(None, "dp", "tensor"),
        P(None, "dp", "tensor"),
        P(None, "dp", "tensor"),
        P(None, "dp", "tensor"),
        P("tensor", "dp"),
        P("tensor", "dp"),
        P("tensor", "dp"),
        P("tensor", "dp"),
    )
    return jax.shard_map(shards, mesh=mesh, in_specs=in_specs, out_specs=out_specs, check_vma=False)
```

```python
import jax
import jax.numpy as jnp
from jax import lax
from jax.experimental import pallas as pl
from jax.experimental.pallas import tpu as pltpu
from jax.sharding import PartitionSpec as P

BETA_ONE = 0.9
BETA_TWO = 0.95
ADAM_EPS = 1e-08
LEARN_RATE = 0.002
CORRECT_ONE = 1.0 - 0.9**10
CORRECT_TWO = 1.0 - 0.95**10

ALL = ("dp", "tensor")
F32 = jnp.float32
BF16 = jnp.bfloat16
VMEM = pl.BlockSpec(memory_space=pltpu.VMEM)
SMEM = pl.BlockSpec(memory_space=pltpu.SMEM)
X_GROUPS = [[hi + 2 * x for x in range(4)] for hi in range(2)]
Y_OFFSETS = (0, 3, 1, 2)


def limit(mebibytes):
    return pltpu.CompilerParams(vmem_limit_bytes=mebibytes * 2**20)


def device_number(x, hi, lo, y, core):
    return (x * 2 + hi) * 32 + lo * 8 + y * 2 + core


def move(value, target):
    pairs = []
    for x in range(4):
        for hi in range(2):
            for lo in range(4):
                for y in range(4):
                    for core in range(2):
                        here = device_number(x, hi, lo, y, core)
                        pairs.append((here, device_number(*target(x, hi, lo, y, core))))
    return lax.ppermute(value, ALL, pairs)


def after(value, *others):
    return lax.optimization_barrier((value, *others))[0]


def along_y(step):
    return lambda x, hi, lo, y, core: (x, hi, lo, (y + step) % 4, core)


def along_lo(step):
    return lambda x, hi, lo, y, core: (x, hi, (lo + step) % 4, y, core)


def other_hi(x, hi, lo, y, core):
    return (x, 1 - hi, lo, y, core)


def other_core(x, hi, lo, y, core):
    return (x, hi, lo, y, 1 - core)


def to_half(x, hi, lo, y, core):
    if hi != y >> 1:
        return (x, 1 - hi, lo, y, core)
    return (x, hi, lo, y ^ 2, core)


def from_half(x, hi, lo, y, core):
    if hi != y >> 1:
        return (x, hi, lo, y ^ 2, core)
    return (x, 1 - hi, lo, y, core)


def power_of_two(expo, sign):
    result = jnp.zeros(expo.shape, F32)
    for level in range(-8, 0):
        result = jnp.where(expo == level, jnp.float32(2.0 ** (sign * level)), result)
    return result


def expand_codes(codes):
    groups = codes.shape[0]
    rows = groups * 4
    spread = (
        (lax.broadcasted_iota(jnp.int32, (rows, groups), 0) >> 2)
        == lax.broadcasted_iota(jnp.int32, (rows, groups), 1)
    ).astype(F32).astype(BF16)
    mask = jnp.full(codes.shape, 12.0, F32)
    for code, bits in enumerate((3.0, 5.0, 9.0, 6.0, 10.0)):
        mask = jnp.where(codes == code, bits, mask)
    mask = jnp.dot(spread, mask.astype(BF16), preferred_element_type=F32).astype(jnp.int32)
    place = lax.broadcasted_iota(jnp.int32, mask.shape, 0) & 3
    return ((mask >> place) & 1) == 1


def quantize(master, keeper, scale, inverse):
    inner = jnp.where(keeper, jnp.clip(master * inverse, -1.0, 1.0), 0.0)
    return inner.astype(BF16) * scale.astype(BF16)


def quantize_kernel(gu_ref, gu_codes, gu_expo, dn_ref, dn_codes, dn_expo, out_ref):
    for part in range(2):
        expo = gu_expo[part : part + 1, :]
        out_ref[part] = quantize(
            gu_ref[part],
            expand_codes(gu_codes[part]),
            power_of_two(expo, 1),
            power_of_two(expo, -1),
        )
    expo = dn_expo[...]
    down = quantize(
        dn_ref[...], expand_codes(dn_codes[...]), power_of_two(expo, 1), power_of_two(expo, -1)
    )
    out_ref[2, :256] = down[:, :256]
    out_ref[2, 256:] = down[:, 256:]


def adam(master, first, second, grad, codes, expo):
    keeper = expand_codes(codes)
    inverse = power_of_two(expo, -1)
    grad = jnp.where(keeper & (jnp.abs(master * inverse) <= 1.0), grad, 0.0)
    first = BETA_ONE * first + (1.0 - BETA_ONE) * grad
    second = BETA_TWO * second + (1.0 - BETA_TWO) * grad * grad
    step = (LEARN_RATE / CORRECT_ONE) * first
    master = master - step / (jnp.sqrt(second * (1.0 / CORRECT_TWO)) + ADAM_EPS)
    return master, first, second, quantize(master, keeper, power_of_two(expo, 1), inverse)


def gu_adam_kernel(grad, master, first, second, codes, expo, new, new_first, new_second, copy):
    which = pl.program_id(0)
    chosen = jnp.where(which == 0, expo[0:1, :], expo[1:2, :])
    result = adam(
        master[0], first[0], second[0], grad[0].astype(F32), codes[0], chosen
    )
    new[0], new_first[0], new_second[0], copy[0] = result


def down_adam_kernel(grad, master, first, second, codes, expo, new, new_first, new_second, copy):
    result = adam(
        master[...],
        first[...],
        second[...],
        jnp.concatenate([grad[0, :256], grad[0, 256:]], axis=1).astype(F32),
        codes[...],
        expo[...],
    )
    new[...], new_first[...], new_second[...], copy[...] = result


def gu_update(grads, master, first, second, codes, expo):
    parts, rows, cols = master.shape
    size = rows
    block = pl.BlockSpec((1, size, cols), lambda i, j: (i, j, 0))
    narrow = pl.BlockSpec((1, size // 4, cols), lambda i, j: (i, j, 0))
    whole = pl.BlockSpec((parts, cols), lambda i, j: (0, 0))
    like = jax.ShapeDtypeStruct(master.shape, F32)
    return pl.pallas_call(
        gu_adam_kernel,
        grid=(parts, 1),
        in_specs=[block, block, block, block, narrow, whole],
        out_specs=[block] * 4,
        out_shape=[like, like, like, jax.ShapeDtypeStruct(master.shape, BF16)],
        name="gu_adam",
    )(grads, master, first, second, codes, expo)


def down_update(grads, master, first, second, codes, expo):
    rows, cols = master.shape
    size = rows
    block = pl.BlockSpec((size, cols), lambda i: (i, 0))
    narrow = pl.BlockSpec((size // 4, cols), lambda i: (i, 0))
    whole = pl.BlockSpec((1, cols), lambda i: (0, 0))
    like = jax.ShapeDtypeStruct(master.shape, F32)
    return pl.pallas_call(
        down_adam_kernel,
        grid=(1,),
        in_specs=[
            pl.BlockSpec((1, cols, size), lambda i: (2, 0, 0)),
            block,
            block,
            block,
            narrow,
            whole,
        ],
        out_specs=[block] * 4,
        out_shape=[like, like, like, jax.ShapeDtypeStruct(master.shape, BF16)],
        name="down_adam",
    )(grads, master, first, second, codes, expo)


def piece_rows(pieces, ring, lo_step, side):
    own, other = pieces
    if ring < 3:
        return jnp.concatenate([own[ring][lo_step, side], other[ring][lo_step, side]], axis=1)
    half, at = lo_step // 2, lo_step % 2
    return jnp.concatenate(
        [own[3 + half][at, side], other[3 + half][at, side]], axis=1
    )


def down_columns(low, core):
    return pl.ds(pl.multiple_of(low * 256, 256), 256), pl.ds(pl.multiple_of(core * 128, 128), 128)


def weight_rows(weights, block, which, low, core):
    start = pl.multiple_of(low * 256 + core * 128, 128)
    second = pl.multiple_of(low * 256 + (1 - core) * 128, 128)
    return jnp.concatenate(
        [weights[block, which, pl.ds(start, 128), :], weights[block, which, pl.ds(second, 128), :]],
        axis=0,
    )


def partial_kernel(mine, place, *refs):
    own, other, weights, out = refs[:5], refs[5:10], refs[10], refs[11]
    acc = refs[12]
    hi, lo, y, core = place[1], place[2], place[3], place[4]
    target = 1 - hi if mine else hi
    acc[...] = jnp.zeros_like(acc)
    for ring, offset in enumerate(Y_OFFSETS):
        from_y = (y + offset) & 3

        @pl.when((from_y >> 1) == target)
        def _():
            for lo_step in range(4):
                block = (lo - lo_step) & 3
                for which in range(2):
                    left = piece_rows((own, other), ring, lo_step, 0)
                    right = weight_rows(weights, block, which, from_y & 1, core)
                    acc[which] += jnp.dot(left, right, preferred_element_type=F32)
                left = piece_rows((own, other), ring, lo_step, 1)
                rows, first = down_columns(from_y & 1, core)
                _, second = down_columns(from_y & 1, 1 - core)
                right = jnp.concatenate(
                    [weights[block, 2, rows, first], weights[block, 2, rows, second]], axis=1
                )
                acc[2] += cross(left, right, 1, 1)

    out[...] = acc[...].astype(out.dtype)


def partial(mine, place, pieces, weights):
    return pl.pallas_call(
        lambda *refs: partial_kernel(mine, *refs),
        in_specs=[SMEM] + [VMEM] * 11,
        out_specs=VMEM,
        out_shape=jax.ShapeDtypeStruct((3, 256, 256), F32 if mine else BF16),
        scratch_shapes=[pltpu.VMEM((3, 256, 256), F32)],
        compiler_params=limit(16),
        name="partial_own" if mine else "partial_sent",
    )(place, *pieces, weights)


def gated_kernel(own, sent, out):
    gate = own[0] + sent[0].astype(F32)
    up = own[1] + sent[1].astype(F32)
    dh = own[2] + sent[2].astype(F32)
    sig = jax.nn.sigmoid(gate)
    act = gate * sig
    out[0] = (dh * up * sig * (1.0 + gate * (1.0 - sig))).astype(BF16)
    out[1] = (dh * act).astype(BF16)
    out[2] = (act * up).astype(BF16)


def gated(own, sent):
    return pl.pallas_call(
        gated_kernel,
        in_specs=[VMEM] * 2,
        out_specs=VMEM,
        out_shape=jax.ShapeDtypeStruct((3, 256, 256), BF16),
        name="gated",
    )(own, sent)


def cross(left, right, left_dim, right_dim):
    return lax.dot_general(
        left, right, (((left_dim,), (right_dim,)), ((), ())), preferred_element_type=F32
    )


def outputs_kernel(sides, place, rows, weights, *outs):
    lo, core = place[2], place[4]
    for side, out in zip(sides, outs):
        to_core = core if side == "kept" else 1 - core
        for low in range(2):
            start = pl.multiple_of(low * 256 + to_core * 128, 128)
            for lo_step in range(4):
                block = (lo + lo_step) & 3
                parts = [weights[block, which, pl.ds(start, 128), :] for which in range(2)]
                down = weights[(block, 2) + down_columns(low, to_core)]
                out[low, lo_step, 0] = cross(rows[2], down, 1, 0).astype(out.dtype)
                out[low, lo_step, 1] = (
                    cross(rows[0], parts[0], 1, 1) + cross(rows[1], parts[1], 1, 1)
                ).astype(out.dtype)


def outputs(sides, place, rows, weights):
    return pl.pallas_call(
        lambda *refs: outputs_kernel(sides, *refs),
        in_specs=[SMEM] + [VMEM] * 2,
        out_specs=[VMEM] * len(sides),
        out_shape=[jax.ShapeDtypeStruct((2, 4, 2, 256, 128), BF16)] * len(sides),
        compiler_params=limit(16),
        name="outputs_" + "_".join(sides),
    )(place, rows, weights)


def combine_kernel(place, own_kept, own_got, arrived_kept, arrived_got, out):
    hi, y = place[1], place[3]
    for step in range(4):
        to_y = (y + step) & 3
        low = to_y & 1

        @pl.when((to_y >> 1) != hi)
        def _():
            out[step] = (own_kept[low].astype(F32) + own_got[low].astype(F32)).astype(BF16)

        @pl.when((to_y >> 1) == hi)
        def _():
            out[step] = (arrived_kept[low].astype(F32) + arrived_got[low].astype(F32)).astype(BF16)


def combine(place, *halves):
    return pl.pallas_call(
        combine_kernel,
        in_specs=[SMEM] + [VMEM] * 4,
        out_specs=VMEM,
        out_shape=jax.ShapeDtypeStruct((4, 4, 2, 256, 128), BF16),
        compiler_params=limit(16),
        name="combine",
    )(place, *halves)


def grads_kernel(own_rows, inverse_scale, place, *refs):
    own, other, rows, out = refs[:5], refs[5:10], refs[10], refs[-1]

    def put(at, value):
        if not own_rows:
            value += refs[11][at].astype(F32)
        out[at] = value.astype(BF16)

    hi, lo, y, core = place[1], place[2], place[3], place[4]
    target = 1 - hi if own_rows else hi
    for ring, offset in enumerate(Y_OFFSETS):
        from_y = (y + offset) & 3

        @pl.when((from_y >> 1) == target)
        def _():
            low = from_y & 1
            first = pl.ds(pl.multiple_of(low * 256 + core * 128, 128), 128)
            second = pl.ds(pl.multiple_of(low * 256 + (1 - core) * 128, 128), 128)
            for lo_step in range(4):
                block = (lo - lo_step) & 3
                left = piece_rows((own, other), ring, lo_step, 0)
                for which in range(2):
                    term = cross(left, rows[which], 0, 0) * inverse_scale
                    put((block, which, first, slice(None)), term[:128])
                    put((block, which, second, slice(None)), term[128:])
                left = piece_rows((own, other), ring, lo_step, 1)
                term = cross(rows[2], left, 0, 0) * inverse_scale
                put((block, 2) + down_columns(low, core), term[:, :128])
                put((block, 2) + down_columns(low, 1 - core), term[:, 128:])


def grads(own_rows, inverse_scale, place, pieces, rows, *before):
    return pl.pallas_call(
        lambda *refs: grads_kernel(own_rows, inverse_scale, *refs),
        in_specs=[SMEM] + [VMEM] * (11 + len(before)),
        out_specs=VMEM,
        out_shape=jax.ShapeDtypeStruct((4, 3, 512, 256), BF16),
        compiler_params=limit(24),
        name="own_grads" if own_rows else "arrived_grads",
    )(place, *pieces, rows, *before)


def gather_pieces(tokens, cotangent, weights):
    start = move(jnp.stack([tokens, cotangent]), to_half)
    line = jnp.stack([start] + [move(start, along_lo(step)) for step in (1, 2, 3)])
    before = move(line, along_y(1))
    after = move(line, along_y(-1))
    far_low = move(before[:2], along_y(1))
    far_high = move(after[2:], along_y(-1))
    far_high, weights = lax.optimization_barrier((far_high, weights))
    own = (line, before, after, far_low, far_high)
    return own + tuple(move(piece, other_core) for piece in own), weights


def scatter_outputs(total):
    f32 = lambda value: value.astype(F32)
    low = move(total[2, :2], along_y(1))
    high = move(total[2, 2:], along_y(-1))
    ahead = jnp.concatenate([(f32(total[1, :2]) + f32(low)).astype(BF16), total[1, 2:]])
    behind = jnp.concatenate([total[3, :2], (f32(total[3, 2:]) + f32(high)).astype(BF16)])
    from_before = move(ahead, along_y(1))
    from_after = move(behind, along_y(-1))
    line = f32(total[0]) + f32(from_before) + f32(from_after)
    leaving = line[1:].astype(BF16)
    result = line[0]
    for step in (1, 2, 3):
        result = result + f32(move(leaving[step - 1], along_lo(step)))
    return result.astype(BF16)


def shards(
    tokens,
    cotangent,
    gu_master,
    gu_first,
    gu_second,
    gu_codes,
    gu_expo,
    down_master,
    down_first,
    down_second,
    down_codes,
    down_expo,
):
    dp, tensor = lax.axis_index("dp"), lax.axis_index("tensor")
    place = jnp.stack([dp >> 1, dp & 1, tensor >> 3, (tensor >> 1) & 3, tensor & 1])
    down_expo = down_expo.reshape(1, -1)
    quant = pl.pallas_call(
        quantize_kernel,
        in_specs=[VMEM] * 6,
        out_specs=VMEM,
        out_shape=jax.ShapeDtypeStruct((3, 512, 256), BF16),
        name="quantize",
    )(gu_master, gu_codes, gu_expo, down_master, down_codes, down_expo)
    weights = lax.all_gather(
        quant.reshape(1536, 256), "dp", axis=0, tiled=True, axis_index_groups=X_GROUPS
    ).reshape(4, 3, 512, 256)
    pieces, weights = gather_pieces(tokens, cotangent, weights)
    sent = partial(False, place, pieces, weights)
    arrived = move(sent, other_hi)
    kept = partial(True, place, pieces, weights)
    rows_own = gated(kept, arrived)
    rows_other = move(rows_own, other_hi)
    inverse_scale = 1.0 / (tokens.shape[0] * lax.axis_size("dp"))
    grad = grads(True, inverse_scale, place, pieces, rows_own)
    rows_own, grad = lax.optimization_barrier((rows_own, grad))
    own_sent, own_kept = outputs(("sent", "kept"), place, rows_own, weights)
    own_got = move(own_sent, other_core)
    rows_other, own_kept = lax.optimization_barrier((rows_other, own_kept))
    grad = grads(False, inverse_scale, place, pieces, rows_other, grad)
    grad = lax.psum_scatter(
        grad.reshape(6144, 256), "dp", scatter_dimension=0, tiled=True, axis_index_groups=X_GROUPS
    ).reshape(3, 512, 256)
    (sent,) = outputs(("sent",), place, rows_other, weights)
    got = move(sent, other_core)
    (kept,) = outputs(("kept",), place, rows_other, weights)
    both = scatter_outputs(combine(place, own_kept, own_got, kept, got))
    gu_new, gu_first_new, gu_second_new, gu_copy = gu_update(
        grad, gu_master, gu_first, gu_second, gu_codes, gu_expo
    )
    down_new, down_first_new, down_second_new, down_copy = down_update(
        grad, down_master, down_first, down_second, down_codes, down_expo
    )
    both = after(move(both, from_half), gu_copy, down_copy)
    return (
        both[0],
        both[1],
        gu_new,
        gu_first_new,
        gu_second_new,
        gu_copy,
        down_new,
        down_first_new,
        down_second_new,
        down_copy,
    )


def solution(mesh):
    in_specs = (
        P("dp", "tensor"),
        P("dp", "tensor"),
        P(None, "dp", "tensor"),
        P(None, "dp", "tensor"),
        P(None, "dp", "tensor"),
        P(None, "dp", "tensor"),
        P(None, "tensor"),
        P("tensor", "dp"),
        P("tensor", "dp"),
        P("tensor", "dp"),
        P("tensor", "dp"),
        P("dp"),
    )
    out_specs = (
        P("dp", "tensor"),
        P("dp", "tensor"),
        P(None, "dp", "tensor"),
        P(None, "dp", "tensor"),
        P(None, "dp", "tensor"),
        P(None, "dp", "tensor"),
        P("tensor", "dp"),
        P("tensor", "dp"),
        P("tensor", "dp"),
        P("tensor", "dp"),
    )
    return jax.shard_map(shards, mesh=mesh, in_specs=in_specs, out_specs=out_specs, check_vma=False)
```

```python
import jax
import jax.numpy as jnp
from jax import lax
from jax.experimental import pallas as pl
from jax.experimental.pallas import tpu as pltpu
from jax.sharding import PartitionSpec as P

BETA_ONE = 0.9
BETA_TWO = 0.95
ADAM_EPS = 1e-08
LEARN_RATE = 0.002
CORRECT_ONE = 1.0 - 0.9**10
CORRECT_TWO = 1.0 - 0.95**10

ALL = ("dp", "tensor")
F32 = jnp.float32
BF16 = jnp.bfloat16
VMEM = pl.BlockSpec(memory_space=pltpu.VMEM)
SMEM = pl.BlockSpec(memory_space=pltpu.SMEM)
X_GROUPS = [[hi + 2 * x for x in range(4)] for hi in range(2)]
Y_OFFSETS = (0, 3, 1, 2)


def limit(mebibytes):
    return pltpu.CompilerParams(vmem_limit_bytes=mebibytes * 2**20)


def device_number(x, hi, lo, y, core):
    return (x * 2 + hi) * 32 + lo * 8 + y * 2 + core


def move(value, target):
    pairs = []
    for x in range(4):
        for hi in range(2):
            for lo in range(4):
                for y in range(4):
                    for core in range(2):
                        here = device_number(x, hi, lo, y, core)
                        pairs.append((here, device_number(*target(x, hi, lo, y, core))))
    return lax.ppermute(value, ALL, pairs)


def after(value, *others):
    return lax.optimization_barrier((value, *others))[0]


def along_y(step):
    return lambda x, hi, lo, y, core: (x, hi, lo, (y + step) % 4, core)


def along_lo(step):
    return lambda x, hi, lo, y, core: (x, hi, (lo + step) % 4, y, core)


def other_hi(x, hi, lo, y, core):
    return (x, 1 - hi, lo, y, core)


def other_core(x, hi, lo, y, core):
    return (x, hi, lo, y, 1 - core)


def to_half(x, hi, lo, y, core):
    if hi != y >> 1:
        return (x, 1 - hi, lo, y, core)
    return (x, hi, lo, y ^ 2, core)


def from_half(x, hi, lo, y, core):
    if hi != y >> 1:
        return (x, hi, lo, y ^ 2, core)
    return (x, 1 - hi, lo, y, core)


def power_of_two(expo, sign):
    result = jnp.zeros(expo.shape, F32)
    for level in range(-8, 0):
        result = jnp.where(expo == level, jnp.float32(2.0 ** (sign * level)), result)
    return result


def expand_codes(codes):
    groups = codes.shape[0]
    rows = groups * 4
    spread = (
        (lax.broadcasted_iota(jnp.int32, (rows, groups), 0) >> 2)
        == lax.broadcasted_iota(jnp.int32, (rows, groups), 1)
    ).astype(F32).astype(BF16)
    mask = jnp.full(codes.shape, 12.0, F32)
    for code, bits in enumerate((3.0, 5.0, 9.0, 6.0, 10.0)):
        mask = jnp.where(codes == code, bits, mask)
    mask = jnp.dot(spread, mask.astype(BF16), preferred_element_type=F32).astype(jnp.int32)
    place = lax.broadcasted_iota(jnp.int32, mask.shape, 0) & 3
    return ((mask >> place) & 1) == 1


def quantize(master, keeper, scale, inverse):
    inner = jnp.where(keeper, jnp.clip(master * inverse, -1.0, 1.0), 0.0)
    return inner.astype(BF16) * scale.astype(BF16)


def quantize_kernel(gu_ref, gu_codes, gu_expo, dn_ref, dn_codes, dn_expo, out_ref):
    for part in range(2):
        expo = gu_expo[part : part + 1, :]
        out_ref[part] = quantize(
            gu_ref[part],
            expand_codes(gu_codes[part]),
            power_of_two(expo, 1),
            power_of_two(expo, -1),
        )
    expo = dn_expo[...]
    down = quantize(
        dn_ref[...], expand_codes(dn_codes[...]), power_of_two(expo, 1), power_of_two(expo, -1)
    )
    out_ref[2, :256] = down[:, :256]
    out_ref[2, 256:] = down[:, 256:]


def adam(master, first, second, grad, codes, expo):
    keeper = expand_codes(codes)
    inverse = power_of_two(expo, -1)
    grad = jnp.where(keeper & (jnp.abs(master * inverse) <= 1.0), grad, 0.0)
    first = BETA_ONE * first + (1.0 - BETA_ONE) * grad
    second = BETA_TWO * second + (1.0 - BETA_TWO) * grad * grad
    step = (LEARN_RATE / CORRECT_ONE) * first
    master = master - step / (jnp.sqrt(second * (1.0 / CORRECT_TWO)) + ADAM_EPS)
    return master, first, second, quantize(master, keeper, power_of_two(expo, 1), inverse)


def gu_adam_kernel(grad, master, first, second, codes, expo, new, new_first, new_second, copy):
    which = pl.program_id(0)
    chosen = jnp.where(which == 0, expo[0:1, :], expo[1:2, :])
    result = adam(
        master[0], first[0], second[0], grad[0].astype(F32), codes[0], chosen
    )
    new[0], new_first[0], new_second[0], copy[0] = result


def down_adam_kernel(grad, master, first, second, codes, expo, new, new_first, new_second, copy):
    result = adam(
        master[...],
        first[...],
        second[...],
        jnp.concatenate([grad[0, :256], grad[0, 256:]], axis=1).astype(F32),
        codes[...],
        expo[...],
    )
    new[...], new_first[...], new_second[...], copy[...] = result


def gu_update(grads, master, first, second, codes, expo):
    parts, rows, cols = master.shape
    size = rows
    block = pl.BlockSpec((1, size, cols), lambda i, j: (i, j, 0))
    narrow = pl.BlockSpec((1, size // 4, cols), lambda i, j: (i, j, 0))
    whole = pl.BlockSpec((parts, cols), lambda i, j: (0, 0))
    like = jax.ShapeDtypeStruct(master.shape, F32)
    return pl.pallas_call(
        gu_adam_kernel,
        grid=(parts, 1),
        in_specs=[block, block, block, block, narrow, whole],
        out_specs=[block] * 4,
        out_shape=[like, like, like, jax.ShapeDtypeStruct(master.shape, BF16)],
        name="gu_adam",
    )(grads, master, first, second, codes, expo)


def down_update(grads, master, first, second, codes, expo):
    rows, cols = master.shape
    size = rows
    block = pl.BlockSpec((size, cols), lambda i: (i, 0))
    narrow = pl.BlockSpec((size // 4, cols), lambda i: (i, 0))
    whole = pl.BlockSpec((1, cols), lambda i: (0, 0))
    like = jax.ShapeDtypeStruct(master.shape, F32)
    return pl.pallas_call(
        down_adam_kernel,
        grid=(1,),
        in_specs=[
            pl.BlockSpec((1, cols, size), lambda i: (2, 0, 0)),
            block,
            block,
            block,
            narrow,
            whole,
        ],
        out_specs=[block] * 4,
        out_shape=[like, like, like, jax.ShapeDtypeStruct(master.shape, BF16)],
        name="down_adam",
    )(grads, master, first, second, codes, expo)


def piece_rows(pieces, ring, lo_step, side):
    own, other = pieces
    if ring < 3:
        return jnp.concatenate([own[ring][lo_step, side], other[ring][lo_step, side]], axis=1)
    half, at = lo_step // 2, lo_step % 2
    return jnp.concatenate(
        [own[3 + half][at, side], other[3 + half][at, side]], axis=1
    )


def down_columns(low, core):
    return pl.ds(pl.multiple_of(low * 256, 256), 256), pl.ds(pl.multiple_of(core * 128, 128), 128)


def weight_rows(weights, block, which, low, core):
    start = pl.multiple_of(low * 256 + core * 128, 128)
    second = pl.multiple_of(low * 256 + (1 - core) * 128, 128)
    return jnp.concatenate(
        [weights[block, which, pl.ds(start, 128), :], weights[block, which, pl.ds(second, 128), :]],
        axis=0,
    )


def partial_kernel(mine, place, *refs):
    own, other, weights, out = refs[:5], refs[5:10], refs[10], refs[11]
    acc = refs[12]
    hi, lo, y, core = place[1], place[2], place[3], place[4]
    target = 1 - hi if mine else hi
    acc[...] = jnp.zeros_like(acc)
    for ring, offset in enumerate(Y_OFFSETS):
        from_y = (y + offset) & 3

        @pl.when((from_y >> 1) == target)
        def _():
            for lo_step in range(4):
                block = (lo - lo_step) & 3
                for which in range(2):
                    left = piece_rows((own, other), ring, lo_step, 0)
                    right = weight_rows(weights, block, which, from_y & 1, core)
                    acc[which] += jnp.dot(left, right, preferred_element_type=F32)
                left = piece_rows((own, other), ring, lo_step, 1)
                rows, first = down_columns(from_y & 1, core)
                _, second = down_columns(from_y & 1, 1 - core)
                right = jnp.concatenate(
                    [weights[block, 2, rows, first], weights[block, 2, rows, second]], axis=1
                )
                acc[2] += cross(left, right, 1, 1)

    out[...] = acc[...].astype(out.dtype)


def partial(mine, place, pieces, weights):
    return pl.pallas_call(
        lambda *refs: partial_kernel(mine, *refs),
        in_specs=[SMEM] + [VMEM] * 11,
        out_specs=VMEM,
        out_shape=jax.ShapeDtypeStruct((3, 256, 256), F32 if mine else BF16),
        scratch_shapes=[pltpu.VMEM((3, 256, 256), F32)],
        compiler_params=limit(16),
        name="partial_own" if mine else "partial_sent",
    )(place, *pieces, weights)


def gated_kernel(own, sent, out):
    gate = own[0] + sent[0].astype(F32)
    up = own[1] + sent[1].astype(F32)
    dh = own[2] + sent[2].astype(F32)
    sig = jax.nn.sigmoid(gate)
    act = gate * sig
    out[0] = (dh * up * sig * (1.0 + gate * (1.0 - sig))).astype(BF16)
    out[1] = (dh * act).astype(BF16)
    out[2] = (act * up).astype(BF16)


def gated(own, sent):
    return pl.pallas_call(
        gated_kernel,
        in_specs=[VMEM] * 2,
        out_specs=VMEM,
        out_shape=jax.ShapeDtypeStruct((3, 256, 256), BF16),
        name="gated",
    )(own, sent)


def cross(left, right, left_dim, right_dim):
    return lax.dot_general(
        left, right, (((left_dim,), (right_dim,)), ((), ())), preferred_element_type=F32
    )


def outputs_kernel(sides, place, rows, weights, *outs):
    lo, core = place[2], place[4]
    for side, out in zip(sides, outs):
        to_core = core if side == "kept" else 1 - core
        for low in range(2):
            start = pl.multiple_of(low * 256 + to_core * 128, 128)
            for lo_step in range(4):
                block = (lo + lo_step) & 3
                parts = [weights[block, which, pl.ds(start, 128), :] for which in range(2)]
                down = weights[(block, 2) + down_columns(low, to_core)]
                out[low, lo_step, 0] = cross(rows[2], down, 1, 0).astype(out.dtype)
                out[low, lo_step, 1] = (
                    cross(rows[0], parts[0], 1, 1) + cross(rows[1], parts[1], 1, 1)
                ).astype(out.dtype)


def outputs(sides, place, rows, weights):
    return pl.pallas_call(
        lambda *refs: outputs_kernel(sides, *refs),
        in_specs=[SMEM] + [VMEM] * 2,
        out_specs=[VMEM] * len(sides),
        out_shape=[jax.ShapeDtypeStruct((2, 4, 2, 256, 128), BF16)] * len(sides),
        compiler_params=limit(16),
        name="outputs_" + "_".join(sides),
    )(place, rows, weights)


def combine_kernel(place, own_kept, own_got, arrived_kept, arrived_got, out):
    hi, y = place[1], place[3]
    for step in range(4):
        to_y = (y + step) & 3
        low = to_y & 1

        @pl.when((to_y >> 1) != hi)
        def _():
            out[step] = (own_kept[low].astype(F32) + own_got[low].astype(F32)).astype(BF16)

        @pl.when((to_y >> 1) == hi)
        def _():
            out[step] = (arrived_kept[low].astype(F32) + arrived_got[low].astype(F32)).astype(BF16)


def combine(place, *halves):
    return pl.pallas_call(
        combine_kernel,
        in_specs=[SMEM] + [VMEM] * 4,
        out_specs=VMEM,
        out_shape=jax.ShapeDtypeStruct((4, 4, 2, 256, 128), BF16),
        compiler_params=limit(16),
        name="combine",
    )(place, *halves)


def grads_kernel(own_rows, inverse_scale, place, *refs):
    own, other, rows, out = refs[:5], refs[5:10], refs[10], refs[-1]

    def put(at, value):
        if not own_rows:
            value += refs[11][at].astype(F32)
        out[at] = value.astype(BF16)

    hi, lo, y, core = place[1], place[2], place[3], place[4]
    target = 1 - hi if own_rows else hi
    for ring, offset in enumerate(Y_OFFSETS):
        from_y = (y + offset) & 3

        @pl.when((from_y >> 1) == target)
        def _():
            low = from_y & 1
            first = pl.ds(pl.multiple_of(low * 256 + core * 128, 128), 128)
            second = pl.ds(pl.multiple_of(low * 256 + (1 - core) * 128, 128), 128)
            for lo_step in range(4):
                block = (lo - lo_step) & 3
                left = piece_rows((own, other), ring, lo_step, 0)
                for which in range(2):
                    term = cross(left, rows[which], 0, 0) * inverse_scale
                    put((block, which, first, slice(None)), term[:128])
                    put((block, which, second, slice(None)), term[128:])
                left = piece_rows((own, other), ring, lo_step, 1)
                term = cross(rows[2], left, 0, 0) * inverse_scale
                put((block, 2) + down_columns(low, core), term[:, :128])
                put((block, 2) + down_columns(low, 1 - core), term[:, 128:])


def grads(own_rows, inverse_scale, place, pieces, rows, *before):
    return pl.pallas_call(
        lambda *refs: grads_kernel(own_rows, inverse_scale, *refs),
        in_specs=[SMEM] + [VMEM] * (11 + len(before)),
        out_specs=VMEM,
        out_shape=jax.ShapeDtypeStruct((4, 3, 512, 256), BF16),
        compiler_params=limit(24),
        name="own_grads" if own_rows else "arrived_grads",
    )(place, *pieces, rows, *before)


def gather_pieces(tokens, cotangent, weights):
    start = move(jnp.stack([tokens, cotangent]), to_half)
    line = jnp.stack([start] + [move(start, along_lo(step)) for step in (1, 2, 3)])
    before = move(line, along_y(1))
    after = move(line, along_y(-1))
    far_low = move(before[:2], along_y(1))
    far_high = move(after[2:], along_y(-1))
    far_high, weights = lax.optimization_barrier((far_high, weights))
    own = (line, before, after, far_low, far_high)
    return own + tuple(move(piece, other_core) for piece in own), weights


def scatter_outputs(total, ready):
    f32 = lambda value: value.astype(F32)
    low = move(total[2, :2], along_y(1))
    high = move(total[2, 2:], along_y(-1))
    ahead = jnp.concatenate([(f32(total[1, :2]) + f32(low)).astype(BF16), total[1, 2:]])
    behind = jnp.concatenate([total[3, :2], (f32(total[3, 2:]) + f32(high)).astype(BF16)])
    from_before = move(ahead, along_y(1))
    from_after = move(behind, along_y(-1))
    line = f32(total[0]) + f32(from_before) + f32(from_after)
    leaving = line[1:].astype(BF16)
    arrived = [move(leaving[step - 1], along_lo(step)) for step in (1, 2, 3)]
    arrived[0], arrived[1], arrived[2], ready = lax.optimization_barrier((*arrived, ready))
    result = line[0]
    for piece in arrived:
        result = result + f32(piece)
    return result.astype(BF16), ready


def shards(
    tokens,
    cotangent,
    gu_master,
    gu_first,
    gu_second,
    gu_codes,
    gu_expo,
    down_master,
    down_first,
    down_second,
    down_codes,
    down_expo,
):
    dp, tensor = lax.axis_index("dp"), lax.axis_index("tensor")
    place = jnp.stack([dp >> 1, dp & 1, tensor >> 3, (tensor >> 1) & 3, tensor & 1])
    down_expo = down_expo.reshape(1, -1)
    quant = pl.pallas_call(
        quantize_kernel,
        in_specs=[VMEM] * 6,
        out_specs=VMEM,
        out_shape=jax.ShapeDtypeStruct((3, 512, 256), BF16),
        name="quantize",
    )(gu_master, gu_codes, gu_expo, down_master, down_codes, down_expo)
    weights = lax.all_gather(
        quant.reshape(1536, 256), "dp", axis=0, tiled=True, axis_index_groups=X_GROUPS
    ).reshape(4, 3, 512, 256)
    pieces, weights = gather_pieces(tokens, cotangent, weights)
    sent = partial(False, place, pieces, weights)
    arrived = move(sent, other_hi)
    kept = partial(True, place, pieces, weights)
    rows_own = gated(kept, arrived)
    rows_other = move(rows_own, other_hi)
    inverse_scale = 1.0 / (tokens.shape[0] * lax.axis_size("dp"))
    grad = grads(True, inverse_scale, place, pieces, rows_own)
    rows_own, grad = lax.optimization_barrier((rows_own, grad))
    own_sent, own_kept = outputs(("sent", "kept"), place, rows_own, weights)
    own_got = move(own_sent, other_core)
    rows_other, own_kept = lax.optimization_barrier((rows_other, own_kept))
    grad = grads(False, inverse_scale, place, pieces, rows_other, grad)
    grad = lax.psum_scatter(
        grad.reshape(6144, 256), "dp", scatter_dimension=0, tiled=True, axis_index_groups=X_GROUPS
    ).reshape(3, 512, 256)
    (sent,) = outputs(("sent",), place, rows_other, weights)
    got = move(sent, other_core)
    (kept,) = outputs(("kept",), place, rows_other, weights)
    down_new, down_first_new, down_second_new, down_copy = down_update(
        grad, down_master, down_first, down_second, down_codes, down_expo
    )
    total = combine(place, own_kept, own_got, got, kept)
    both, down_copy = scatter_outputs(total, down_copy)
    gu_new, gu_first_new, gu_second_new, gu_copy = gu_update(
        grad, gu_master, gu_first, gu_second, gu_codes, gu_expo
    )
    both = after(move(both, from_half), gu_copy)
    return (
        both[0],
        both[1],
        gu_new,
        gu_first_new,
        gu_second_new,
        gu_copy,
        down_new,
        down_first_new,
        down_second_new,
        down_copy,
    )


def solution(mesh):
    in_specs = (
        P("dp", "tensor"),
        P("dp", "tensor"),
        P(None, "dp", "tensor"),
        P(None, "dp", "tensor"),
        P(None, "dp", "tensor"),
        P(None, "dp", "tensor"),
        P(None, "tensor"),
        P("tensor", "dp"),
        P("tensor", "dp"),
        P("tensor", "dp"),
        P("tensor", "dp"),
        P("dp"),
    )
    out_specs = (
        P("dp", "tensor"),
        P("dp", "tensor"),
        P(None, "dp", "tensor"),
        P(None, "dp", "tensor"),
        P(None, "dp", "tensor"),
        P(None, "dp", "tensor"),
        P("tensor", "dp"),
        P("tensor", "dp"),
        P("tensor", "dp"),
        P("tensor", "dp"),
    )
    return jax.shard_map(shards, mesh=mesh, in_specs=in_specs, out_specs=out_specs, check_vma=False)
```

```python
import jax
import jax.numpy as jnp
from jax import lax
from jax.experimental import pallas as pl
from jax.experimental.pallas import tpu as pltpu
from jax.sharding import PartitionSpec as P

BETA_ONE = 0.9
BETA_TWO = 0.95
ADAM_EPS = 1e-08
LEARN_RATE = 0.002
CORRECT_ONE = 1.0 - 0.9**10
CORRECT_TWO = 1.0 - 0.95**10

ALL = ("dp", "tensor")
F32 = jnp.float32
BF16 = jnp.bfloat16
VMEM = pl.BlockSpec(memory_space=pltpu.VMEM)
SMEM = pl.BlockSpec(memory_space=pltpu.SMEM)
X_GROUPS = [[hi + 2 * x for x in range(4)] for hi in range(2)]
Y_OFFSETS = (0, 3, 1, 2)


def limit(mebibytes):
    return pltpu.CompilerParams(vmem_limit_bytes=mebibytes * 2**20)


def device_number(x, hi, lo, y, core):
    return (x * 2 + hi) * 32 + lo * 8 + y * 2 + core


def move(value, target):
    pairs = []
    for x in range(4):
        for hi in range(2):
            for lo in range(4):
                for y in range(4):
                    for core in range(2):
                        here = device_number(x, hi, lo, y, core)
                        pairs.append((here, device_number(*target(x, hi, lo, y, core))))
    return lax.ppermute(value, ALL, pairs)


def after(value, *others):
    return lax.optimization_barrier((value, *others))[0]


def along_y(step):
    return lambda x, hi, lo, y, core: (x, hi, lo, (y + step) % 4, core)


def along_lo(step):
    return lambda x, hi, lo, y, core: (x, hi, (lo + step) % 4, y, core)


def other_hi(x, hi, lo, y, core):
    return (x, 1 - hi, lo, y, core)


def other_core(x, hi, lo, y, core):
    return (x, hi, lo, y, 1 - core)


def to_half(x, hi, lo, y, core):
    if hi != y >> 1:
        return (x, 1 - hi, lo, y, core)
    return (x, hi, lo, y ^ 2, core)


def from_half(x, hi, lo, y, core):
    if hi != y >> 1:
        return (x, hi, lo, y ^ 2, core)
    return (x, 1 - hi, lo, y, core)


def power_of_two(expo, sign):
    result = jnp.zeros(expo.shape, F32)
    for level in range(-8, 0):
        result = jnp.where(expo == level, jnp.float32(2.0 ** (sign * level)), result)
    return result


def expand_codes(codes):
    groups = codes.shape[0]
    rows = groups * 4
    spread = (
        (lax.broadcasted_iota(jnp.int32, (rows, groups), 0) >> 2)
        == lax.broadcasted_iota(jnp.int32, (rows, groups), 1)
    ).astype(F32).astype(BF16)
    mask = jnp.full(codes.shape, 12.0, F32)
    for code, bits in enumerate((3.0, 5.0, 9.0, 6.0, 10.0)):
        mask = jnp.where(codes == code, bits, mask)
    mask = jnp.dot(spread, mask.astype(BF16), preferred_element_type=F32).astype(jnp.int32)
    place = lax.broadcasted_iota(jnp.int32, mask.shape, 0) & 3
    return ((mask >> place) & 1) == 1


def quantize(master, keeper, scale, inverse):
    inner = jnp.where(keeper, jnp.clip(master * inverse, -1.0, 1.0), 0.0)
    return inner.astype(BF16) * scale.astype(BF16)


def quantize_kernel(gu_ref, gu_codes, gu_expo, dn_ref, dn_codes, dn_expo, out_ref):
    for part in range(2):
        expo = gu_expo[part : part + 1, :]
        out_ref[part] = quantize(
            gu_ref[part],
            expand_codes(gu_codes[part]),
            power_of_two(expo, 1),
            power_of_two(expo, -1),
        )
    expo = dn_expo[...]
    down = quantize(
        dn_ref[...], expand_codes(dn_codes[...]), power_of_two(expo, 1), power_of_two(expo, -1)
    )
    out_ref[2, :256] = down[:, :256]
    out_ref[2, 256:] = down[:, 256:]


def adam(master, first, second, grad, codes, expo):
    keeper = expand_codes(codes)
    inverse = power_of_two(expo, -1)
    grad = jnp.where(keeper & (jnp.abs(master * inverse) <= 1.0), grad, 0.0)
    first = BETA_ONE * first + (1.0 - BETA_ONE) * grad
    second = BETA_TWO * second + (1.0 - BETA_TWO) * grad * grad
    step = (LEARN_RATE / CORRECT_ONE) * first
    master = master - step / (jnp.sqrt(second * (1.0 / CORRECT_TWO)) + ADAM_EPS)
    return master, first, second, quantize(master, keeper, power_of_two(expo, 1), inverse)


def gu_adam_kernel(grad, master, first, second, codes, expo, new, new_first, new_second, copy):
    which = pl.program_id(0)
    chosen = jnp.where(which == 0, expo[0:1, :], expo[1:2, :])
    result = adam(
        master[0], first[0], second[0], grad[0].astype(F32), codes[0], chosen
    )
    new[0], new_first[0], new_second[0], copy[0] = result


def down_adam_kernel(grad, master, first, second, codes, expo, new, new_first, new_second, copy):
    result = adam(
        master[...],
        first[...],
        second[...],
        jnp.concatenate([grad[0, :256], grad[0, 256:]], axis=1).astype(F32),
        codes[...],
        expo[...],
    )
    new[...], new_first[...], new_second[...], copy[...] = result


def gu_update(grads, master, first, second, codes, expo):
    parts, rows, cols = master.shape
    size = rows
    block = pl.BlockSpec((1, size, cols), lambda i, j: (i, j, 0))
    narrow = pl.BlockSpec((1, size // 4, cols), lambda i, j: (i, j, 0))
    whole = pl.BlockSpec((parts, cols), lambda i, j: (0, 0))
    like = jax.ShapeDtypeStruct(master.shape, F32)
    return pl.pallas_call(
        gu_adam_kernel,
        grid=(parts, 1),
        in_specs=[block, block, block, block, narrow, whole],
        out_specs=[block] * 4,
        out_shape=[like, like, like, jax.ShapeDtypeStruct(master.shape, BF16)],
        name="gu_adam",
    )(grads, master, first, second, codes, expo)


def down_update(grads, master, first, second, codes, expo):
    rows, cols = master.shape
    size = rows
    block = pl.BlockSpec((size, cols), lambda i: (i, 0))
    narrow = pl.BlockSpec((size // 4, cols), lambda i: (i, 0))
    whole = pl.BlockSpec((1, cols), lambda i: (0, 0))
    like = jax.ShapeDtypeStruct(master.shape, F32)
    return pl.pallas_call(
        down_adam_kernel,
        grid=(1,),
        in_specs=[
            pl.BlockSpec((1, cols, size), lambda i: (2, 0, 0)),
            block,
            block,
            block,
            narrow,
            whole,
        ],
        out_specs=[block] * 4,
        out_shape=[like, like, like, jax.ShapeDtypeStruct(master.shape, BF16)],
        name="down_adam",
    )(grads, master, first, second, codes, expo)


def piece_rows(pieces, ring, lo_step, side):
    own, other = pieces
    if ring < 3:
        return jnp.concatenate([own[ring][lo_step, side], other[ring][lo_step, side]], axis=1)
    half, at = lo_step // 2, lo_step % 2
    return jnp.concatenate(
        [own[3 + half][at, side], other[3 + half][at, side]], axis=1
    )


def down_columns(low, core):
    return pl.ds(pl.multiple_of(low * 256, 256), 256), pl.ds(pl.multiple_of(core * 128, 128), 128)


def weight_rows(weights, block, which, low, core):
    start = pl.multiple_of(low * 256 + core * 128, 128)
    second = pl.multiple_of(low * 256 + (1 - core) * 128, 128)
    return jnp.concatenate(
        [weights[block, which, pl.ds(start, 128), :], weights[block, which, pl.ds(second, 128), :]],
        axis=0,
    )


def partial_kernel(mine, place, *refs):
    own, other, weights, out = refs[:5], refs[5:10], refs[10], refs[11]
    acc = refs[12]
    hi, lo, y, core = place[1], place[2], place[3], place[4]
    target = 1 - hi if mine else hi
    acc[...] = jnp.zeros_like(acc)
    for ring, offset in enumerate(Y_OFFSETS):
        from_y = (y + offset) & 3

        @pl.when((from_y >> 1) == target)
        def _():
            for lo_step in range(4):
                block = (lo - lo_step) & 3
                for which in range(2):
                    left = piece_rows((own, other), ring, lo_step, 0)
                    right = weight_rows(weights, block, which, from_y & 1, core)
                    acc[which] += jnp.dot(left, right, preferred_element_type=F32)
                left = piece_rows((own, other), ring, lo_step, 1)
                rows, first = down_columns(from_y & 1, core)
                _, second = down_columns(from_y & 1, 1 - core)
                right = jnp.concatenate(
                    [weights[block, 2, rows, first], weights[block, 2, rows, second]], axis=1
                )
                acc[2] += cross(left, right, 1, 1)

    out[...] = acc[...].astype(out.dtype)


def partial(mine, place, pieces, weights):
    return pl.pallas_call(
        lambda *refs: partial_kernel(mine, *refs),
        in_specs=[SMEM] + [VMEM] * 11,
        out_specs=VMEM,
        out_shape=jax.ShapeDtypeStruct((3, 256, 256), F32 if mine else BF16),
        scratch_shapes=[pltpu.VMEM((3, 256, 256), F32)],
        compiler_params=limit(16),
        name="partial_own" if mine else "partial_sent",
    )(place, *pieces, weights)


def gated_kernel(own, sent, out):
    gate = own[0] + sent[0].astype(F32)
    up = own[1] + sent[1].astype(F32)
    dh = own[2] + sent[2].astype(F32)
    sig = jax.nn.sigmoid(gate)
    act = gate * sig
    out[0] = (dh * up * sig * (1.0 + gate * (1.0 - sig))).astype(BF16)
    out[1] = (dh * act).astype(BF16)
    out[2] = (act * up).astype(BF16)


def gated(own, sent):
    return pl.pallas_call(
        gated_kernel,
        in_specs=[VMEM] * 2,
        out_specs=VMEM,
        out_shape=jax.ShapeDtypeStruct((3, 256, 256), BF16),
        name="gated",
    )(own, sent)


def cross(left, right, left_dim, right_dim):
    return lax.dot_general(
        left, right, (((left_dim,), (right_dim,)), ((), ())), preferred_element_type=F32
    )


def outputs_kernel(sides, place, rows, weights, *outs):
    lo, core = place[2], place[4]
    for side, out in zip(sides, outs):
        to_core = core if side == "kept" else 1 - core
        for low in range(2):
            start = pl.multiple_of(low * 256 + to_core * 128, 128)
            for lo_step in range(4):
                block = (lo + lo_step) & 3
                parts = [weights[block, which, pl.ds(start, 128), :] for which in range(2)]
                down = weights[(block, 2) + down_columns(low, to_core)]
                out[low, lo_step, 0] = cross(rows[2], down, 1, 0).astype(out.dtype)
                out[low, lo_step, 1] = (
                    cross(rows[0], parts[0], 1, 1) + cross(rows[1], parts[1], 1, 1)
                ).astype(out.dtype)


def outputs(sides, place, rows, weights):
    return pl.pallas_call(
        lambda *refs: outputs_kernel(sides, *refs),
        in_specs=[SMEM] + [VMEM] * 2,
        out_specs=[VMEM] * len(sides),
        out_shape=[jax.ShapeDtypeStruct((2, 4, 2, 256, 128), BF16)] * len(sides),
        compiler_params=limit(16),
        name="outputs_" + "_".join(sides),
    )(place, rows, weights)


def combine_kernel(place, own_kept, own_got, arrived_kept, arrived_got, out):
    hi, y = place[1], place[3]
    for step in range(4):
        to_y = (y + step) & 3
        low = to_y & 1

        @pl.when((to_y >> 1) != hi)
        def _():
            out[step] = (own_kept[low].astype(F32) + own_got[low].astype(F32)).astype(BF16)

        @pl.when((to_y >> 1) == hi)
        def _():
            out[step] = (arrived_kept[low].astype(F32) + arrived_got[low].astype(F32)).astype(BF16)


def combine(place, *halves):
    return pl.pallas_call(
        combine_kernel,
        in_specs=[SMEM] + [VMEM] * 4,
        out_specs=VMEM,
        out_shape=jax.ShapeDtypeStruct((4, 4, 2, 256, 128), BF16),
        compiler_params=limit(16),
        name="combine",
    )(place, *halves)


def grads_kernel(own_rows, inverse_scale, place, *refs):
    own, other, rows, out = refs[:5], refs[5:10], refs[10], refs[-1]

    def put(at, value):
        if not own_rows:
            value += refs[11][at].astype(F32)
        out[at] = value.astype(BF16)

    hi, lo, y, core = place[1], place[2], place[3], place[4]
    target = 1 - hi if own_rows else hi
    for ring, offset in enumerate(Y_OFFSETS):
        from_y = (y + offset) & 3

        @pl.when((from_y >> 1) == target)
        def _():
            low = from_y & 1
            first = pl.ds(pl.multiple_of(low * 256 + core * 128, 128), 128)
            second = pl.ds(pl.multiple_of(low * 256 + (1 - core) * 128, 128), 128)
            for lo_step in range(4):
                block = (lo - lo_step) & 3
                left = piece_rows((own, other), ring, lo_step, 0)
                for which in range(2):
                    term = cross(left, rows[which], 0, 0) * inverse_scale
                    put((block, which, first, slice(None)), term[:128])
                    put((block, which, second, slice(None)), term[128:])
                left = piece_rows((own, other), ring, lo_step, 1)
                term = cross(rows[2], left, 0, 0) * inverse_scale
                put((block, 2) + down_columns(low, core), term[:, :128])
                put((block, 2) + down_columns(low, 1 - core), term[:, 128:])


def grads(own_rows, inverse_scale, place, pieces, rows, *before):
    return pl.pallas_call(
        lambda *refs: grads_kernel(own_rows, inverse_scale, *refs),
        in_specs=[SMEM] + [VMEM] * (11 + len(before)),
        out_specs=VMEM,
        out_shape=jax.ShapeDtypeStruct((4, 3, 512, 256), BF16),
        compiler_params=limit(24),
        name="own_grads" if own_rows else "arrived_grads",
    )(place, *pieces, rows, *before)


def gather_pieces(tokens, cotangent, weights):
    start = move(jnp.stack([tokens, cotangent]), to_half)
    line = jnp.stack([start] + [move(start, along_lo(step)) for step in (1, 2, 3)])
    before = move(line, along_y(1))
    after = move(line, along_y(-1))
    far_low = move(before[:2], along_y(1))
    far_high = move(after[2:], along_y(-1))
    far_high, weights = lax.optimization_barrier((far_high, weights))
    own = (line, before, after, far_low, far_high)
    return own + tuple(move(piece, other_core) for piece in own), weights


def scatter_outputs(total, ready):
    f32 = lambda value: value.astype(F32)
    low = move(total[2, :2], along_y(1))
    high = move(total[2, 2:], along_y(-1))
    ahead = jnp.concatenate([(f32(total[1, :2]) + f32(low)).astype(BF16), total[1, 2:]])
    behind = jnp.concatenate([total[3, :2], (f32(total[3, 2:]) + f32(high)).astype(BF16)])
    from_before = move(ahead, along_y(1))
    from_after = move(behind, along_y(-1))
    line = f32(total[0]) + f32(from_before) + f32(from_after)
    leaving = line[1:].astype(BF16)
    arrived = [move(leaving[step - 1], along_lo(step)) for step in (1, 2, 3)]
    arrived[0], arrived[1], arrived[2], ready = lax.optimization_barrier((*arrived, ready))
    result = line[0]
    for piece in arrived:
        result = result + f32(piece)
    return result.astype(BF16), ready


def shards(
    tokens,
    cotangent,
    gu_master,
    gu_first,
    gu_second,
    gu_codes,
    gu_expo,
    down_master,
    down_first,
    down_second,
    down_codes,
    down_expo,
):
    dp, tensor = lax.axis_index("dp"), lax.axis_index("tensor")
    place = jnp.stack([dp >> 1, dp & 1, tensor >> 3, (tensor >> 1) & 3, tensor & 1])
    down_expo = down_expo.reshape(1, -1)
    quant = pl.pallas_call(
        quantize_kernel,
        in_specs=[VMEM] * 6,
        out_specs=VMEM,
        out_shape=jax.ShapeDtypeStruct((3, 512, 256), BF16),
        name="quantize",
    )(gu_master, gu_codes, gu_expo, down_master, down_codes, down_expo)
    weights = lax.all_gather(
        quant.reshape(1536, 256), "dp", axis=0, tiled=True, axis_index_groups=X_GROUPS
    ).reshape(4, 3, 512, 256)
    pieces, weights = gather_pieces(tokens, cotangent, weights)
    sent = partial(False, place, pieces, weights)
    arrived = move(sent, other_hi)
    kept = partial(True, place, pieces, weights)
    rows_own = gated(kept, arrived)
    rows_other = move(rows_own, other_hi)
    inverse_scale = 1.0 / (tokens.shape[0] * lax.axis_size("dp"))
    grad = grads(True, inverse_scale, place, pieces, rows_own)
    own_sent, own_kept = outputs(("sent", "kept"), place, rows_own, weights)
    own_got = move(own_sent, other_core)
    grad = grads(False, inverse_scale, place, pieces, rows_other, grad)
    grad = lax.psum_scatter(
        grad.reshape(6144, 256), "dp", scatter_dimension=0, tiled=True, axis_index_groups=X_GROUPS
    ).reshape(3, 512, 256)
    (sent,) = outputs(("sent",), place, rows_other, weights)
    got = move(sent, other_core)
    (kept,) = outputs(("kept",), place, rows_other, weights)
    down_new, down_first_new, down_second_new, down_copy = down_update(
        grad, down_master, down_first, down_second, down_codes, down_expo
    )
    total = combine(place, own_kept, own_got, got, kept)
    both, down_copy = scatter_outputs(total, down_copy)
    gu_new, gu_first_new, gu_second_new, gu_copy = gu_update(
        grad, gu_master, gu_first, gu_second, gu_codes, gu_expo
    )
    both = after(move(both, from_half), gu_copy)
    return (
        both[0],
        both[1],
        gu_new,
        gu_first_new,
        gu_second_new,
        gu_copy,
        down_new,
        down_first_new,
        down_second_new,
        down_copy,
    )


def solution(mesh):
    in_specs = (
        P("dp", "tensor"),
        P("dp", "tensor"),
        P(None, "dp", "tensor"),
        P(None, "dp", "tensor"),
        P(None, "dp", "tensor"),
        P(None, "dp", "tensor"),
        P(None, "tensor"),
        P("tensor", "dp"),
        P("tensor", "dp"),
        P("tensor", "dp"),
        P("tensor", "dp"),
        P("dp"),
    )
    out_specs = (
        P("dp", "tensor"),
        P("dp", "tensor"),
        P(None, "dp", "tensor"),
        P(None, "dp", "tensor"),
        P(None, "dp", "tensor"),
        P(None, "dp", "tensor"),
        P("tensor", "dp"),
        P("tensor", "dp"),
        P("tensor", "dp"),
        P("tensor", "dp"),
    )
    return jax.shard_map(shards, mesh=mesh, in_specs=in_specs, out_specs=out_specs, check_vma=False)
```
